32 devices in a mesh: layer: 4 (over x, core), feat: 8 (over z, y).
Axes of the slice: x: 2, y: 2, z: 4, core: 2. Of those that a mesh axis runs over, the one named last changes fastest.
Arguments:
- activations: bfloat16 [64, 4, 2304], P('feat', 'layer'), may hold values from -6 to 6
- enc_weight: bfloat16 [4, 2304, 8192], P('layer', None, 'feat'), may hold values from -0.0625 to 0.0625
- dec_weight: bfloat16 [4, 8192, 2304], P('layer', 'feat'), may hold values from -0.09375 to 0.09375
- enc_bias: float32 [8192], P('feat'), may hold values from -3 to 3
- threshold: float32 [8192], P('feat'), may hold values from 0.1 to 1
- dec_bias: float32 [4, 2304], P('layer'), may hold values from -3 to 3
- token_mask: int32 [64], replicated, may hold values 0 or 1
Outputs:
- squared_error: float32 [64, 4], P('feat', 'layer')
- latent_grad: float32 [64, 8192], P(None, 'feat')
- input_grad: bfloat16 [64, 4, 2304], P('feat', 'layer')
The draws below stay inside these ranges and needn't reach their ends.
All inputs are finite; a program needn't handle non-finite values.
Results may differ from the reference program's by a relative error of at most 0.015.
Values may be sent and summed in bfloat16 or wider, within the bound.
No kernel may reach another device: no remote copies, remote signals or barrier semaphores. Data moves between devices by JAX's collectives and lax.ppermute only.
A program may use at most 64 MiB of HBM per device.

```python
import math
import jax
import jax.numpy as jnp

D = 2304
LAYERS = 4
FEATURES = 8192
TOKENS = 64


def set_ends(result, rng, smallest, largest):
    spot = [jax.random.randint(jax.random.fold_in(rng, axis), (), 0, length) for axis, length in enumerate(result.shape)]
    longest = result.shape.index(max(result.shape))
    next_to = spot[:longest] + [(spot[longest] + 1) % result.shape[longest]] + spot[longest + 1:]
    return result.at[tuple(spot)].set(smallest).at[tuple(next_to)].set(largest)


def shard_levels(key, shape, shards, smallest, largest):
    def one(axis_at, blocks):
        draws = jax.random.uniform(jax.random.fold_in(jax.random.fold_in(key, 6), axis_at), (blocks,), jnp.float32, smallest / len(shards), largest / len(shards))
        return jnp.repeat(jnp.exp(draws), shape[axis_at] // blocks).reshape((-1,) + (1,) * (len(shape) - axis_at - 1))

    gain = one(*shards[0])
    for cut in shards[1:]:
        gain = gain * one(*cut)
    return gain


def scatter_about(key, extent, deviation, bound, split=(), held_as=jnp.bfloat16):
    factor_of = shard_levels(key, extent, split, -0.22, 0.18) if split else 1.0
    result = jax.random.normal(key, extent, jnp.float32) * deviation * factor_of
    return jnp.minimum(jnp.maximum(result, -bound), bound).astype(held_as)


def setup_inputs(seed: int = 0) -> dict:
    key_of = jax.random.split(jax.random.key(seed), 8)
    return {
        "activations": scatter_about(key_of[0], (TOKENS, LAYERS, D), 1.0, 6.0, ((0, 8), (1, 4))),
        "enc_weight": scatter_about(key_of[1], (LAYERS, D, FEATURES), (LAYERS * D) ** -0.5, 0.0625, ((0, 4), (2, 8))),
        "dec_weight": scatter_about(key_of[2], (LAYERS, FEATURES, D), (FEATURES // 2) ** -0.5, 0.09375, ((0, 4), (1, 8))),
        "enc_bias": scatter_about(key_of[3], (FEATURES,), 0.5, 3.0, ((0, 8),), jnp.float32),
        "threshold": jnp.clip(jnp.exp(math.log(1.0) - 2.3025851 * jax.random.uniform(key_of[4], (FEATURES,), jnp.float32) ** shard_levels(key_of[4], (FEATURES,), ((0, 8),), -0.2, 0.2)), 0.1, 1.0),
        "dec_bias": scatter_about(key_of[5], (LAYERS, D), 0.5, 3.0, ((0, 4),), jnp.float32),
        "token_mask": set_ends((jax.random.randint(key_of[6], (TOKENS,), 0, 4) < 3).astype(jnp.int32), jax.random.fold_in(key_of[6], 1), 0, 1),
    }


jump_scale = 0.25


def reference(activations, enc_weight, dec_weight, enc_bias, threshold, dec_bias, token_mask):
    acts_wide = activations.astype(jnp.float32)
    enc_wide = enc_weight.astype(jnp.float32)
    dec_wide = dec_weight.astype(jnp.float32)
    preact = jnp.einsum('tld,ldf->tf', acts_wide, enc_wide) + enc_bias
    gating = jax.nn.sigmoid((preact - threshold) / jump_scale)
    latent = (preact * gating).astype(jnp.bfloat16)
    gate_slope = gating + preact * gating * (1.0 - gating) / jump_scale
    rebuilt = jnp.einsum('tf,lfd->tld', latent.astype(jnp.float32), dec_wide)
    weights_mask = token_mask.astype(jnp.float32)[:, None, None]
    error = weights_mask * (rebuilt + dec_bias[None, :, :] - acts_wide)
    squared_error = jnp.mean(error * error, axis=-1)
    error_half = error.astype(jnp.bfloat16)
    latent_grad = jnp.einsum('tld,lfd->tf', error_half.astype(jnp.float32), dec_wide)
    preact_grad = (latent_grad * gate_slope).astype(jnp.bfloat16)
    grad_terms = jnp.einsum('tf,ldf->tld', preact_grad.astype(jnp.float32), enc_wide)
    input_grad = (grad_terms - error).astype(jnp.bfloat16)
    return squared_error, latent_grad, input_grad
```

```python
import jax
import jax.numpy as jnp
from jax import lax
from jax.sharding import PartitionSpec as P

jump_scale = 0.25


def spread(block, axis):
    n = lax.axis_size(axis)
    pieces = lax.all_to_all(jnp.broadcast_to(block[None], (n, *block.shape)), axis, 0, 0)
    return pieces.reshape(n * block.shape[0], *block.shape[1:])


def sum_scatter(terms, axis):
    n = lax.axis_size(axis)
    pieces = lax.all_to_all(terms.astype(jnp.bfloat16).reshape(n, -1, terms.shape[-1]), axis, 0, 0)
    return jnp.sum(pieces.astype(jnp.float32), axis=0)


def sum_all(terms, axis):
    return jnp.sum(lax.all_gather(terms.astype(jnp.bfloat16), axis).astype(jnp.float32), axis=0)


def dot(a, b, dims):
    return lax.dot_general(a, b, (dims, ((), ())), preferred_element_type=jnp.float32)


def shards(activations, enc_weight, dec_weight, enc_bias, threshold, dec_bias, token_mask):
    tok_dev = activations.shape[0]
    enc, dec = enc_weight[0], dec_weight[0]
    acts = activations[:, 0]
    whole_acts = spread(acts, "feat")
    preact = sum_all(dot(whole_acts, enc, ((1,), (0,))), "layer") + enc_bias
    gating = jax.nn.sigmoid((preact - threshold) / jump_scale)
    latent = (preact * gating).astype(jnp.bfloat16)
    gate_slope = gating + preact * gating * (1.0 - gating) / jump_scale
    rebuilt = sum_scatter(dot(latent, dec, ((1,), (0,))), "feat")
    mask = lax.dynamic_slice_in_dim(token_mask, lax.axis_index("feat") * tok_dev, tok_dev)
    error = mask.astype(jnp.float32)[:, None] * (rebuilt + dec_bias - acts.astype(jnp.float32))
    error_all = spread(error.astype(jnp.bfloat16), "feat")
    squared_error = jnp.mean(error * error, axis=-1, keepdims=True)
    latent_grad = sum_all(dot(error_all, dec, ((1,), (1,))), "layer")
    preact_grad = (latent_grad * gate_slope).astype(jnp.bfloat16)
    grad_terms = sum_scatter(dot(preact_grad, enc, ((1,), (1,))), "feat")
    input_grad = (grad_terms - error).astype(jnp.bfloat16)
    return (squared_error, latent_grad, input_grad[:, None])


def solution(mesh):
    return jax.shard_map(
        shards,
        mesh=mesh,
        in_specs=(
            P("feat", "layer", None),
            P("layer", None, "feat"),
            P("layer", "feat", None),
            P("feat"),
            P("feat"),
            P("layer", None),
            P(),
        ),
        out_specs=(P("feat", "layer"), P(None, "feat"), P("feat", "layer", None)),
        check_vma=False,
    )
```

```python
import functools

import jax
import jax.numpy as jnp
from jax import lax
from jax.experimental import pallas as pl
from jax.experimental.pallas import tpu as pltpu
from jax.sharding import PartitionSpec as P

jump_scale = 0.25
columns = 256
half, wide = jnp.bfloat16, jnp.float32


def near(shape, dtype):
    return pltpu.VMEM(shape, dtype)


def free(shape, dtype):
    return jax.ShapeDtypeStruct(shape, dtype)


def call(body, outs, *args, scratch=(), fetched=0, sent=0):
    here, away = pl.BlockSpec(memory_space=pltpu.VMEM), pl.BlockSpec(memory_space=pl.ANY)
    spaces = [pltpu.HBM] * fetched + [pltpu.VMEM] * (len(args) - fetched)
    return pl.pallas_call(
        body,
        out_shape=outs,
        in_specs=[away] * fetched + [here] * (len(args) - fetched),
        out_specs=[here] * (len(outs) - sent) + [away] * sent,
        scratch_shapes=scratch,
        compiler_params=pltpu.CompilerParams(vmem_limit_bytes=16 << 20),
    )(*map(pltpu.with_memory_space_constraint, args, spaces))


def rows_of(ref):
    return ref[...].reshape(-1, ref.shape[-1])


def begin(block, enc_bias, threshold, enc, dec, copies, bias_near, threshold_near, done):
    n = copies.shape[0]
    moves = [(block, copies.at[i]) for i in range(n)] + [(enc_bias, bias_near), (threshold, threshold_near)]
    moves = [pltpu.make_async_copy(here, there, done.at[i]) for i, (here, there) in enumerate(moves)]
    for move in moves:
        move.start()
    for move in moves:
        move.wait()


def encode(acts, weight, out):
    x = rows_of(acts)
    for at in range(0, out.shape[1], columns):
        out[:, at : at + columns] = jnp.dot(
            x, weight[:, at : at + columns], preferred_element_type=wide
        ).astype(half)


def encode_turned(rows, weight, out):
    x = rows_of(rows)
    for at in range(0, out.shape[1], columns):
        out[:, at : at + columns] = lax.dot_general(
            x, weight[at : at + columns, :], (((1,), (1,)), ((), ())), preferred_element_type=wide
        ).astype(half)


def decode(terms, enc_bias, threshold, weight, out, slope):
    preact = jnp.sum(terms[...].astype(wide), axis=0) + enc_bias[...]
    gating = jax.nn.sigmoid((preact - threshold[...]) / jump_scale)
    slope[...] = gating + preact * gating * (1.0 - gating) / jump_scale
    latent = (preact * gating).astype(half)
    for at in range(0, out.shape[1], columns):
        out[:, at : at + columns] = jnp.dot(
            latent, weight[:, at : at + columns], preferred_element_type=wide
        ).astype(half)


def decode_turned(terms, slope, weight, out, result, total, done):
    latent_grad = jnp.sum(terms[...].astype(wide), axis=0)
    total[...] = latent_grad
    move = pltpu.make_async_copy(total, result, done)
    move.start()
    x = (latent_grad * slope[...]).astype(half)
    for at in range(0, out.shape[1], columns):
        out[:, at : at + columns] = lax.dot_general(
            x, weight[at : at + columns, :], (((1,), (1,)), ((), ())), preferred_element_type=wide
        ).astype(half)
    move.wait()


def compare(terms, dec_bias, acts, token_mask, error, copies, squared):
    rows, tokens = error.shape[0], token_mask.shape[1]
    token = lax.axis_index("feat") * rows + lax.broadcasted_iota(jnp.int32, (rows, tokens), 0)
    own = token == lax.broadcasted_iota(jnp.int32, (rows, tokens), 1)
    mask = jnp.sum(jnp.where(own, token_mask[...].astype(wide), 0.0), axis=1, keepdims=True)
    rebuilt = jnp.sum(terms[...].astype(wide), axis=0)
    found = mask * (rebuilt + dec_bias[...] - acts[...].astype(wide))
    error[...] = found
    copies[...] = jnp.broadcast_to(found.astype(half)[None], copies.shape)
    means = jnp.mean(found * found, axis=1, keepdims=True)
    one = lax.broadcasted_iota(jnp.int32, (rows, rows), 0) == lax.broadcasted_iota(jnp.int32, (rows, rows), 1)
    squared[...] = jnp.sum(jnp.where(one, means, 0.0), axis=0, keepdims=True)


def finish(terms, error, squared, out, squared_out):
    squared_out[...] = squared[...]
    out[...] = (jnp.sum(terms[...].astype(wide), axis=0) - error[...]).astype(half)


def shards(activations, enc_weight, dec_weight, enc_bias, threshold, dec_bias, token_mask):
    n_feat = lax.axis_size("feat")
    tok_dev, _, depth = activations.shape
    tokens, width = n_feat * tok_dev, enc_bias.shape[0]
    enc, dec = enc_weight[0], dec_weight[0]
    acts = activations[:, 0]
    exchange = functools.partial(lax.all_to_all, axis_name="feat", split_axis=0, concat_axis=0)
    by_owner = (n_feat, tok_dev, depth)

    copies, enc_bias, threshold = call(
        begin,
        [near(by_owner, half), near((1, width), wide), near((1, width), wide)],
        acts,
        enc_bias[None],
        threshold[None],
        enc,
        dec,
        scratch=[pltpu.SemaphoreType.DMA((n_feat + 2,))],
        fetched=5,
    )
    whole_acts = exchange(copies)
    [terms] = call(encode, [near((tokens, width), half)], whole_acts, enc)
    terms = lax.all_gather(terms, "layer")
    decoded, slope = call(
        decode,
        [near((tokens, depth), half), near((tokens, width), wide)],
        terms,
        enc_bias,
        threshold,
        dec,
    )
    pieces = exchange(decoded.reshape(by_owner))
    error, copies, squared = call(
        compare,
        [near((tok_dev, depth), wide), near(by_owner, half), near((1, tok_dev), wide)],
        pieces,
        dec_bias,
        acts,
        token_mask[None],
    )
    error_all = exchange(copies)
    [terms] = call(encode_turned, [near((tokens, width), half)], error_all, dec)
    terms = lax.all_gather(terms, "layer")
    grads, latent_grad = call(
        decode_turned,
        [near((tokens, depth), half), free((tokens, width), wide)],
        terms,
        slope,
        enc,
        scratch=[pltpu.VMEM((tokens, width), wide), pltpu.SemaphoreType.DMA],
        sent=1,
    )
    pieces = exchange(grads.reshape(by_owner))
    input_grad, squared = call(
        finish, [free((tok_dev, depth), half), free((1, tok_dev), wide)], pieces, error, squared
    )
    return (squared.T, latent_grad, input_grad[:, None])


def solution(mesh):
    return jax.shard_map(
        shards,
        mesh=mesh,
        in_specs=(
            P("feat", "layer", None),
            P("layer", None, "feat"),
            P("layer", "feat", None),
            P("feat"),
            P("feat"),
            P("layer", None),
            P(),
        ),
        out_specs=(P("feat", "layer"), P(None, "feat"), P("feat", "layer", None)),
        check_vma=False,
    )
```

```python
import functools

import jax
import jax.numpy as jnp
from jax import lax
from jax.experimental import pallas as pl
from jax.experimental.pallas import tpu as pltpu
from jax.sharding import PartitionSpec as P

jump_scale = 0.25
columns = 256
half, wide = jnp.bfloat16, jnp.float32


def near(shape, dtype):
    return pltpu.VMEM(shape, dtype)


def free(shape, dtype):
    return jax.ShapeDtypeStruct(shape, dtype)


def call(body, outs, *args, scratch=(), fetched=0, sent=0):
    here, away = pl.BlockSpec(memory_space=pltpu.VMEM), pl.BlockSpec(memory_space=pl.ANY)
    spaces = [pltpu.HBM] * fetched + [pltpu.VMEM] * (len(args) - fetched)
    return pl.pallas_call(
        body,
        out_shape=outs,
        in_specs=[away] * fetched + [here] * (len(args) - fetched),
        out_specs=[here] * (len(outs) - sent) + [away] * sent,
        scratch_shapes=scratch,
        compiler_params=pltpu.CompilerParams(vmem_limit_bytes=16 << 20),
    )(*map(pltpu.with_memory_space_constraint, args, spaces))


def add(one, other, out):
    out[...] = (one[...].astype(wide) + other[...].astype(wide)).astype(half)


def swap_sums(terms, axis):
    n, span = lax.axis_size(axis), 1
    while True:
        other = lax.ppermute(terms, axis, [(i, i ^ span) for i in range(n)])
        span *= 2
        if span == n:
            return terms, other
        [terms] = call(add, [near(terms.shape, half)], terms, other)


def rows_of(ref):
    return ref[...].reshape(-1, ref.shape[-1])


def begin(block, enc_bias, threshold, enc, dec, copies, bias_near, threshold_near, done):
    n = copies.shape[0]
    moves = [(block, copies.at[i]) for i in range(n)] + [(enc_bias, bias_near), (threshold, threshold_near)]
    moves = [pltpu.make_async_copy(here, there, done.at[i]) for i, (here, there) in enumerate(moves)]
    for move in moves:
        move.start()
    for move in moves:
        move.wait()


def encode(acts, weight, out):
    x = rows_of(acts)
    for at in range(0, out.shape[1], columns):
        out[:, at : at + columns] = jnp.dot(
            x, weight[:, at : at + columns], preferred_element_type=wide
        ).astype(half)


def encode_turned(rows, weight, out):
    x = rows_of(rows)
    for at in range(0, out.shape[1], columns):
        out[:, at : at + columns] = lax.dot_general(
            x, weight[at : at + columns, :], (((1,), (1,)), ((), ())), preferred_element_type=wide
        ).astype(half)


def decode(terms, others, enc_bias, threshold, weight, out, slope):
    preact = terms[...].astype(wide) + others[...].astype(wide) + enc_bias[...]
    gating = jax.nn.sigmoid((preact - threshold[...]) / jump_scale)
    slope[...] = gating + preact * gating * (1.0 - gating) / jump_scale
    latent = (preact * gating).astype(half)
    for at in range(0, out.shape[1], columns):
        out[:, at : at + columns] = jnp.dot(
            latent, weight[:, at : at + columns], preferred_element_type=wide
        ).astype(half)


def decode_turned(terms, others, slope, weight, out, result, total, done):
    latent_grad = terms[...].astype(wide) + others[...].astype(wide)
    total[...] = latent_grad
    move = pltpu.make_async_copy(total, result, done)
    move.start()
    x = (latent_grad * slope[...]).astype(half)
    for at in range(0, out.shape[1], columns):
        out[:, at : at + columns] = lax.dot_general(
            x, weight[at : at + columns, :], (((1,), (1,)), ((), ())), preferred_element_type=wide
        ).astype(half)
    move.wait()


def compare(terms, dec_bias, acts, token_mask, error, copies, squared):
    rows, tokens = error.shape[0], token_mask.shape[1]
    token = lax.axis_index("feat") * rows + lax.broadcasted_iota(jnp.int32, (rows, tokens), 0)
    own = token == lax.broadcasted_iota(jnp.int32, (rows, tokens), 1)
    mask = jnp.sum(jnp.where(own, token_mask[...].astype(wide), 0.0), axis=1, keepdims=True)
    rebuilt = jnp.sum(terms[...].astype(wide), axis=0)
    found = mask * (rebuilt + dec_bias[...] - acts[...].astype(wide))
    error[...] = found
    copies[...] = jnp.broadcast_to(found.astype(half)[None], copies.shape)
    means = jnp.mean(found * found, axis=1, keepdims=True)
    one = lax.broadcasted_iota(jnp.int32, (rows, rows), 0) == lax.broadcasted_iota(jnp.int32, (rows, rows), 1)
    squared[...] = jnp.sum(jnp.where(one, means, 0.0), axis=0, keepdims=True)


def finish(terms, error, squared, out, squared_out):
    squared_out[...] = squared[...]
    out[...] = (jnp.sum(terms[...].astype(wide), axis=0) - error[...]).astype(half)


def shards(activations, enc_weight, dec_weight, enc_bias, threshold, dec_bias, token_mask):
    n_feat = lax.axis_size("feat")
    tok_dev, _, depth = activations.shape
    tokens, width = n_feat * tok_dev, enc_bias.shape[0]
    enc, dec = enc_weight[0], dec_weight[0]
    acts = activations[:, 0]
    exchange = functools.partial(lax.all_to_all, axis_name="feat", split_axis=0, concat_axis=0)
    by_owner = (n_feat, tok_dev, depth)

    copies, enc_bias, threshold = call(
        begin,
        [near(by_owner, half), near((1, width), wide), near((1, width), wide)],
        acts,
        enc_bias[None],
        threshold[None],
        enc,
        dec,
        scratch=[pltpu.SemaphoreType.DMA((n_feat + 2,))],
        fetched=5,
    )
    whole_acts = exchange(copies)
    [terms] = call(encode, [near((tokens, width), half)], whole_acts, enc)
    terms, others = swap_sums(terms, "layer")
    decoded, slope = call(
        decode,
        [near((tokens, depth), half), near((tokens, width), wide)],
        terms,
        others,
        enc_bias,
        threshold,
        dec,
    )
    pieces = exchange(decoded.reshape(by_owner))
    error, copies, squared = call(
        compare,
        [near((tok_dev, depth), wide), near(by_owner, half), near((1, tok_dev), wide)],
        pieces,
        dec_bias,
        acts,
        token_mask[None],
    )
    error_all = exchange(copies)
    [terms] = call(encode_turned, [near((tokens, width), half)], error_all, dec)
    terms, others = swap_sums(terms, "layer")
    grads, latent_grad = call(
        decode_turned,
        [near((tokens, depth), half), free((tokens, width), wide)],
        terms,
        others,
        slope,
        enc,
        scratch=[pltpu.VMEM((tokens, width), wide), pltpu.SemaphoreType.DMA],
        sent=1,
    )
    pieces = exchange(grads.reshape(by_owner))
    input_grad, squared = call(
        finish, [free((tok_dev, depth), half), free((1, tok_dev), wide)], pieces, error, squared
    )
    return (squared.T, latent_grad, input_grad[:, None])


def solution(mesh):
    return jax.shard_map(
        shards,
        mesh=mesh,
        in_specs=(
            P("feat", "layer", None),
            P("layer", None, "feat"),
            P("layer", "feat", None),
            P("feat"),
            P("feat"),
            P("layer", None),
            P(),
        ),
        out_specs=(P("feat", "layer"), P(None, "feat"), P("feat", "layer", None)),
        check_vma=False,
    )
```

```python
import functools

import jax
import jax.numpy as jnp
from jax import lax
from jax.experimental import pallas as pl
from jax.experimental.pallas import tpu as pltpu
from jax.sharding import PartitionSpec as P

jump_scale = 0.25
columns = 256
half, wide = jnp.bfloat16, jnp.float32


def near(shape, dtype):
    return pltpu.VMEM(shape, dtype)


def free(shape, dtype):
    return jax.ShapeDtypeStruct(shape, dtype)


def call(body, outs, *args, scratch=(), fetched=0, sent=0, work=False, same={}):
    here, away = pl.BlockSpec(memory_space=pltpu.VMEM), pl.BlockSpec(memory_space=pl.ANY)
    size = sum(a.size * a.dtype.itemsize for a in args)
    cost = pl.CostEstimate(flops=0, transcendentals=0, bytes_accessed=2 * size) if work else None
    spaces = [pltpu.HBM] * fetched + [pltpu.VMEM] * (len(args) - fetched)
    return pl.pallas_call(
        body,
        out_shape=outs,
        in_specs=[away] * fetched + [here] * (len(args) - fetched),
        out_specs=[here] * (len(outs) - sent) + [away] * sent,
        scratch_shapes=scratch,
        compiler_params=pltpu.CompilerParams(vmem_limit_bytes=16 << 20),
        cost_estimate=cost,
        input_output_aliases=same,
    )(*map(pltpu.with_memory_space_constraint, args, spaces))


def add(one, other, out):
    out[...] = (one[...].astype(wide) + other[...].astype(wide)).astype(half)


def swap_sums(terms, axis, weight):
    n, span = lax.axis_size(axis), 1
    while True:
        other = lax.ppermute(terms, axis, [(i, i ^ span) for i in range(n)])
        span *= 2
        if span == n:
            [turned] = call(turn, [near(weight.shape[::-1], half)], weight, terms, work=True)
            return terms, other, turned
        [terms] = call(add, [near(terms.shape, half)], terms, other)


def rows_of(ref):
    return ref[...].reshape(-1, ref.shape[-1])


def encode(acts, weight, out):
    x = rows_of(acts)
    for at in range(0, out.shape[1], columns):
        out[:, at : at + columns] = jnp.dot(
            x, weight[:, at : at + columns], preferred_element_type=wide
        ).astype(half)


def encode_first(enc_bias, threshold, acts, weight, out, bias_near, threshold_near, done):
    moves = [
        pltpu.make_async_copy(enc_bias, bias_near, done.at[0]),
        pltpu.make_async_copy(threshold, threshold_near, done.at[1]),
    ]
    for move in moves:
        move.start()
    encode(acts, weight, out)
    for move in moves:
        move.wait()


def turn(weight, after, out):
    for at in range(0, weight.shape[0], columns):
        out[:, at : at + columns] = weight[at : at + columns, :].T


def decode(terms, others, enc_bias, threshold, weight, before, out, slope):
    preact = terms[...].astype(wide) + others[...].astype(wide) + enc_bias[...]
    gating = jax.nn.sigmoid((preact - threshold[...]) / jump_scale)
    slope[...] = gating + preact * gating * (1.0 - gating) / jump_scale
    latent = (preact * gating).astype(half)
    for at in range(0, out.shape[1], columns):
        out[:, at : at + columns] = jnp.dot(
            latent, weight[:, at : at + columns], preferred_element_type=wide
        ).astype(half)


def decode_grad(terms, others, slope, weight, out, total):
    latent_grad = terms[...].astype(wide) + others[...].astype(wide)
    total[...] = latent_grad
    x = (latent_grad * slope[...]).astype(half)
    for at in range(0, out.shape[1], columns):
        out[:, at : at + columns] = jnp.dot(
            x, weight[:, at : at + columns], preferred_element_type=wide
        ).astype(half)


def compare(terms, dec_bias, acts, token_mask, error, copies, squared):
    rows, tokens = error.shape[0], token_mask.shape[1]
    token = lax.axis_index("feat") * rows + lax.broadcasted_iota(jnp.int32, (rows, tokens), 0)
    own = token == lax.broadcasted_iota(jnp.int32, (rows, tokens), 1)
    mask = jnp.sum(jnp.where(own, token_mask[...].astype(wide), 0.0), axis=1, keepdims=True)
    rebuilt = jnp.sum(terms[...].astype(wide), axis=0)
    found = mask * (rebuilt + dec_bias[...] - acts[...].astype(wide))
    error[...] = found
    copies[...] = jnp.broadcast_to(found.astype(half)[None], copies.shape)
    means = jnp.mean(found * found, axis=1, keepdims=True)
    one = lax.broadcasted_iota(jnp.int32, (rows, rows), 0) == lax.broadcasted_iota(jnp.int32, (rows, rows), 1)
    squared[...] = jnp.sum(jnp.where(one, means, 0.0), axis=0, keepdims=True)


def finish(terms, error, squared, total, out, squared_out, total_out, held, done):
    moves = [(total, total_out), (squared, squared_out), (held, out)]
    moves = [pltpu.make_async_copy(here, there, done.at[i]) for i, (here, there) in enumerate(moves)]
    moves[0].start()
    moves[1].start()
    held[...] = (jnp.sum(terms[...].astype(wide), axis=0) - error[...]).astype(half)
    moves[2].start()
    for move in moves:
        move.wait()


def shards(activations, enc_weight, dec_weight, enc_bias, threshold, dec_bias, token_mask):
    n_feat = lax.axis_size("feat")
    tok_dev, _, depth = activations.shape
    tokens, width = n_feat * tok_dev, enc_bias.shape[0]
    enc, dec = enc_weight[0], dec_weight[0]
    acts = activations[:, 0]
    exchange = functools.partial(lax.all_to_all, axis_name="feat", split_axis=0, concat_axis=0)
    by_owner = (n_feat, tok_dev, depth)

    copies = jnp.broadcast_to(acts[None], by_owner)
    [copies] = call(lambda *refs: None, [near(by_owner, half)], enc, dec, copies, fetched=2, same={2: 0})
    whole_acts = exchange(copies)
    terms, enc_bias, threshold = call(
        encode_first,
        [near((tokens, width), half), near((1, width), wide), near((1, width), wide)],
        enc_bias[None],
        threshold[None],
        whole_acts,
        enc,
        scratch=[pltpu.SemaphoreType.DMA((2,))],
        fetched=2,
    )
    terms, others, dec_turned = swap_sums(terms, "layer", dec)
    decoded, slope = call(
        decode,
        [near((tokens, depth), half), near((tokens, width), wide)],
        terms,
        others,
        enc_bias,
        threshold,
        dec,
        dec_turned,
    )
    pieces = exchange(decoded.reshape(by_owner))
    error, copies, squared = call(
        compare,
        [near((tok_dev, depth), wide), near(by_owner, half), near((1, tok_dev), wide)],
        pieces,
        dec_bias,
        acts,
        token_mask[None],
    )
    error_all = exchange(copies)
    [terms] = call(encode, [near((tokens, width), half)], error_all, dec_turned)
    terms, others, enc_turned = swap_sums(terms, "layer", enc)
    grads, latent_grad = call(
        decode_grad,
        [near((tokens, depth), half), near((tokens, width), wide)],
        terms,
        others,
        slope,
        enc_turned,
    )
    pieces = exchange(grads.reshape(by_owner))
    input_grad, squared, latent_grad = call(
        finish,
        [free((tok_dev, depth), half), free((1, tok_dev), wide), free((tokens, width), wide)],
        pieces,
        error,
        squared,
        latent_grad,
        scratch=[pltpu.VMEM((tok_dev, depth), half), pltpu.SemaphoreType.DMA((3,))],
        sent=3,
    )
    return (squared.T, latent_grad, input_grad[:, None])


def solution(mesh):
    return jax.shard_map(
        shards,
        mesh=mesh,
        in_specs=(
            P("feat", "layer", None),
            P("layer", None, "feat"),
            P("layer", "feat", None),
            P("feat"),
            P("feat"),
            P("layer", None),
            P(),
        ),
        out_specs=(P("feat", "layer"), P(None, "feat"), P("feat", "layer", None)),
        check_vma=False,
    )
```

```python
import functools

import jax
import jax.numpy as jnp
from jax import lax
from jax.experimental import pallas as pl
from jax.experimental.pallas import tpu as pltpu
from jax.sharding import PartitionSpec as P

jump_scale = 0.25
columns = 256
half, wide = jnp.bfloat16, jnp.float32


def near(shape, dtype):
    return pltpu.VMEM(shape, dtype)


def free(shape, dtype):
    return jax.ShapeDtypeStruct(shape, dtype)


def call(body, outs, *args, scratch=(), fetched=0, sent=0, work=False, same={}):
    here, away = pl.BlockSpec(memory_space=pltpu.VMEM), pl.BlockSpec(memory_space=pl.ANY)
    size = sum(a.size * a.dtype.itemsize for a in args)
    cost = pl.CostEstimate(flops=0, transcendentals=0, bytes_accessed=2 * size) if work else None
    spaces = [pltpu.HBM] * fetched + [pltpu.VMEM] * (len(args) - fetched)
    return pl.pallas_call(
        body,
        out_shape=outs,
        in_specs=[away] * fetched + [here] * (len(args) - fetched),
        out_specs=[here] * (len(outs) - sent) + [away] * sent,
        scratch_shapes=scratch,
        compiler_params=pltpu.CompilerParams(vmem_limit_bytes=16 << 20),
        cost_estimate=cost,
        input_output_aliases=same,
    )(*map(pltpu.with_memory_space_constraint, args, spaces))


def add(one, other, out):
    out[...] = (one[...].astype(wide) + other[...].astype(wide)).astype(half)


def swap_sums(terms, axis, weight):
    n, span = lax.axis_size(axis), 1
    while True:
        other = lax.ppermute(terms, axis, [(i, i ^ span) for i in range(n)])
        span *= 2
        if span == n:
            [turned] = call(turn, [near(weight.shape[::-1], half)], weight, terms, work=True)
            return terms, other, turned
        [terms] = call(add, [near(terms.shape, half)], terms, other)


def rows_of(ref):
    return ref[...].reshape(-1, ref.shape[-1])


def encode(acts, weight, out):
    x = rows_of(acts)
    for at in range(0, out.shape[1], columns):
        out[:, at : at + columns] = jnp.dot(
            x, weight[:, at : at + columns], preferred_element_type=wide
        ).astype(half)


def encode_first(enc_bias, threshold, acts, weight, out, bias_near, threshold_near, done):
    moves = [
        pltpu.make_async_copy(enc_bias, bias_near, done.at[0]),
        pltpu.make_async_copy(threshold, threshold_near, done.at[1]),
    ]
    for move in moves:
        move.start()
    encode(acts, weight, out)
    for move in moves:
        move.wait()


def encode_paired(block, rows, weight, out):
    x = rows_of(rows)
    places = paired(out.shape[0] // block, block)
    for at in range(0, out.shape[1], columns):
        found = jnp.dot(x, weight[:, at : at + columns], preferred_element_type=wide)
        found = jnp.concatenate([found[place] for place in places])
        out[:, at : at + columns] = found.astype(half)


def turn(weight, after, out):
    for at in range(0, weight.shape[0], columns):
        out[:, at : at + columns] = weight[at : at + columns, :].T


def paired(n, block):
    at = [(2 * (i % (n // 2)) + i // (n // 2)) * block for i in range(n)]
    return [slice(first, first + block) for first in at]


def decode(block, terms, others, enc_bias, threshold, weight, before, out, slope):
    preact = terms[...].astype(wide) + others[...].astype(wide) + enc_bias[...]
    gating = jax.nn.sigmoid((preact - threshold[...]) / jump_scale)
    slope[...] = gating + preact * gating * (1.0 - gating) / jump_scale
    n = out.shape[0] // block
    latent = preact * gating
    order = [i for first in range(n // 2) for i in (first, first + n // 2)]
    latent = jnp.concatenate([latent[i * block : (i + 1) * block] for i in order]).astype(half)
    for at in range(0, out.shape[1], columns):
        out[:, at : at + columns] = jnp.dot(
            latent, weight[:, at : at + columns], preferred_element_type=wide
        ).astype(half)


def decode_grad(terms, others, slope, weight, out, total):
    latent_grad = terms[...].astype(wide) + others[...].astype(wide)
    total[...] = latent_grad
    x = (latent_grad * slope[...]).astype(half)
    for at in range(0, out.shape[1], columns):
        out[:, at : at + columns] = jnp.dot(
            x, weight[:, at : at + columns], preferred_element_type=wide
        ).astype(half)


def add_up(terms, out, sent):
    found = jnp.sum(terms[...].astype(wide), axis=0)
    out[...] = found
    sent[...] = found.astype(half)


def compare(one, other, dec_bias, acts, token_mask, error, copies, squared, held):
    n, rows, _ = acts.shape
    tokens = token_mask.shape[1]
    me = lax.axis_index("feat")
    place, upper = lax.rem(me, n // 2), me // (n // 2)
    row = lax.broadcasted_iota(jnp.int32, (2 * rows, tokens), 0)
    token = jnp.where(row < rows, place * rows + row, (place + n // 2) * rows + row - rows)
    own = token == lax.broadcasted_iota(jnp.int32, (2 * rows, tokens), 1)
    mask = jnp.sum(jnp.where(own, token_mask[...].astype(wide), 0.0), axis=1, keepdims=True)
    here = jnp.concatenate([acts[place].astype(wide), acts[place + n // 2].astype(wide)])
    held[...] = mask * (one[...] + other[...].astype(wide) + dec_bias[...] - here)
    copies[...] = jnp.broadcast_to(held[...].astype(half)[None], copies.shape)
    found = held[pl.ds(pl.multiple_of(upper * rows, rows), rows), :]
    error[...] = found
    means = jnp.mean(found * found, axis=1, keepdims=True)
    one = lax.broadcasted_iota(jnp.int32, (rows, rows), 0) == lax.broadcasted_iota(jnp.int32, (rows, rows), 1)
    squared[...] = jnp.sum(jnp.where(one, means, 0.0), axis=0, keepdims=True)


def finish(terms, error, squared, total, out, squared_out, total_out, held, done):
    moves = [(total, total_out), (squared, squared_out), (held, out)]
    moves = [pltpu.make_async_copy(here, there, done.at[i]) for i, (here, there) in enumerate(moves)]
    moves[0].start()
    moves[1].start()
    held[...] = (jnp.sum(terms[...].astype(wide), axis=0) - error[...]).astype(half)
    moves[2].start()
    for move in moves:
        move.wait()


def shards(activations, enc_weight, dec_weight, enc_bias, threshold, dec_bias, token_mask):
    n_feat = lax.axis_size("feat")
    tok_dev, _, depth = activations.shape
    tokens, width = n_feat * tok_dev, enc_bias.shape[0]
    enc, dec = enc_weight[0], dec_weight[0]
    acts = activations[:, 0]
    exchange = functools.partial(lax.all_to_all, axis_name="feat", split_axis=0, concat_axis=0)
    by_owner = (n_feat, tok_dev, depth)

    copies = jnp.broadcast_to(acts[None], by_owner)
    [copies] = call(lambda *refs: None, [near(by_owner, half)], enc, dec, copies, fetched=2, same={2: 0})
    whole_acts = exchange(copies)
    terms, enc_bias, threshold = call(
        encode_first,
        [near((tokens, width), half), near((1, width), wide), near((1, width), wide)],
        enc_bias[None],
        threshold[None],
        whole_acts,
        enc,
        scratch=[pltpu.SemaphoreType.DMA((2,))],
        fetched=2,
    )
    terms, others, dec_turned = swap_sums(terms, "layer", dec)
    decoded, slope = call(
        functools.partial(decode, tok_dev),
        [near((tokens, depth), half), near((tokens, width), wide)],
        terms,
        others,
        enc_bias,
        threshold,
        dec,
        dec_turned,
    )
    by_pair = (n_feat // 2, 2 * tok_dev, depth)
    halves = [list(range(n_feat // 2)), list(range(n_feat // 2, n_feat))]
    pieces = exchange(decoded.reshape(by_pair), axis_index_groups=halves)
    one, other = call(add_up, [near(by_pair[1:], wide), near(by_pair[1:], half)], pieces)
    other = lax.ppermute(other, "feat", [(i, (i + n_feat // 2) % n_feat) for i in range(n_feat)])
    error, copies, squared = call(
        compare,
        [near((tok_dev, depth), wide), near(by_pair, half), near((1, tok_dev), wide)],
        one,
        other,
        dec_bias,
        whole_acts,
        token_mask[None],
        scratch=[pltpu.VMEM(by_pair[1:], wide)],
    )
    error_all = exchange(copies, axis_index_groups=halves)
    [terms] = call(
        functools.partial(encode_paired, tok_dev), [near((tokens, width), half)], error_all, dec_turned
    )
    terms, others, enc_turned = swap_sums(terms, "layer", enc)
    grads, latent_grad = call(
        decode_grad,
        [near((tokens, depth), half), near((tokens, width), wide)],
        terms,
        others,
        slope,
        enc_turned,
    )
    pieces = exchange(grads.reshape(by_owner))
    input_grad, squared, latent_grad = call(
        finish,
        [free((tok_dev, depth), half), free((1, tok_dev), wide), free((tokens, width), wide)],
        pieces,
        error,
        squared,
        latent_grad,
        scratch=[pltpu.VMEM((tok_dev, depth), half), pltpu.SemaphoreType.DMA((3,))],
        sent=3,
    )
    return (squared.T, latent_grad, input_grad[:, None])


def solution(mesh):
    return jax.shard_map(
        shards,
        mesh=mesh,
        in_specs=(
            P("feat", "layer", None),
            P("layer", None, "feat"),
            P("layer", "feat", None),
            P("feat"),
            P("feat"),
            P("layer", None),
            P(),
        ),
        out_specs=(P("feat", "layer"), P(None, "feat"), P("feat", "layer", None)),
        check_vma=False,
    )
```

```python
import functools

import jax
import jax.numpy as jnp
from jax import lax
from jax.experimental import pallas as pl
from jax.experimental.pallas import tpu as pltpu
from jax.sharding import PartitionSpec as P

jump_scale = 0.25
columns = 256
half, wide = jnp.bfloat16, jnp.float32


def near(shape, dtype):
    return pltpu.VMEM(shape, dtype)


def free(shape, dtype):
    return jax.ShapeDtypeStruct(shape, dtype)


def call(body, outs, *args, scratch=(), fetched=0, sent=0, work=False, same={}):
    here, away = pl.BlockSpec(memory_space=pltpu.VMEM), pl.BlockSpec(memory_space=pl.ANY)
    size = sum(a.size * a.dtype.itemsize for a in args)
    cost = pl.CostEstimate(flops=0, transcendentals=0, bytes_accessed=2 * size) if work else None
    spaces = [pltpu.HBM] * fetched + [pltpu.VMEM] * (len(args) - fetched)
    return pl.pallas_call(
        body,
        out_shape=outs,
        in_specs=[away] * fetched + [here] * (len(args) - fetched),
        out_specs=[here] * (len(outs) - sent) + [away] * sent,
        scratch_shapes=scratch,
        compiler_params=pltpu.CompilerParams(vmem_limit_bytes=16 << 20),
        cost_estimate=cost,
        input_output_aliases=same,
    )(*map(pltpu.with_memory_space_constraint, args, spaces))


def add(one, other, out):
    out[...] = (one[...].astype(wide) + other[...].astype(wide)).astype(half)


def swap_sums(terms, axis, weight):
    n, span = lax.axis_size(axis), 1
    while True:
        other = lax.ppermute(terms, axis, [(i, i ^ span) for i in range(n)])
        span *= 2
        if span == n:
            [turned] = call(turn, [near(weight.shape[::-1], half)], weight, terms, work=True)
            return terms, other, turned
        [terms] = call(add, [near(terms.shape, half)], terms, other)


def rows_of(ref):
    return ref[...].reshape(-1, ref.shape[-1])


def encode_first(block, enc_bias, threshold, acts, weight, out, bias_near, threshold_near, done):
    moves = [
        pltpu.make_async_copy(enc_bias, bias_near, done.at[0]),
        pltpu.make_async_copy(threshold, threshold_near, done.at[1]),
    ]
    for move in moves:
        move.start()
    encode_paired(block, acts, weight, out)
    for move in moves:
        move.wait()


def encode_paired(block, rows, weight, out):
    x = rows_of(rows)
    places = paired(out.shape[0] // block, block)
    for at in range(0, out.shape[1], columns):
        found = jnp.dot(x, weight[:, at : at + columns], preferred_element_type=wide)
        found = jnp.concatenate([found[place] for place in places])
        out[:, at : at + columns] = found.astype(half)


def turn(weight, after, out):
    for at in range(0, weight.shape[0], columns):
        out[:, at : at + columns] = weight[at : at + columns, :].T


def paired(n, block):
    at = [(2 * (i % (n // 2)) + i // (n // 2)) * block for i in range(n)]
    return [slice(first, first + block) for first in at]


def decode(block, terms, others, enc_bias, threshold, weight, before, out, slope):
    preact = terms[...].astype(wide) + others[...].astype(wide) + enc_bias[...]
    gating = jax.nn.sigmoid((preact - threshold[...]) / jump_scale)
    slope[...] = gating + preact * gating * (1.0 - gating) / jump_scale
    n = out.shape[0] // block
    latent = preact * gating
    order = [i for first in range(n // 2) for i in (first, first + n // 2)]
    latent = jnp.concatenate([latent[i * block : (i + 1) * block] for i in order]).astype(half)
    for at in range(0, out.shape[1], columns):
        out[:, at : at + columns] = jnp.dot(
            latent, weight[:, at : at + columns], preferred_element_type=wide
        ).astype(half)


def decode_grad(terms, others, slope, weight, out, total):
    latent_grad = terms[...].astype(wide) + others[...].astype(wide)
    total[...] = latent_grad
    x = (latent_grad * slope[...]).astype(half)
    for at in range(0, out.shape[1], columns):
        out[:, at : at + columns] = jnp.dot(
            x, weight[:, at : at + columns], preferred_element_type=wide
        ).astype(half)


def bring(far, out, done):
    move = pltpu.make_async_copy(far, out, done)
    move.start()
    move.wait()


def join(acts, other, copies):
    first = lax.axis_index("feat") < lax.axis_size("feat") // 2
    mine, theirs = acts[...].astype(wide), other[...].astype(wide)
    both = jnp.concatenate([jnp.where(first, mine, theirs), jnp.where(first, theirs, mine)]).astype(half)
    copies[...] = jnp.broadcast_to(both[None], copies.shape)


def add_up(terms, out, sent):
    found = jnp.sum(terms[...].astype(wide), axis=0)
    out[...] = found
    sent[...] = found.astype(half)


def compare(one, other, dec_bias, acts, token_mask, error, copies, squared, held):
    n, rows = 2 * acts.shape[0], acts.shape[1] // 2
    tokens = token_mask.shape[1]
    me = lax.axis_index("feat")
    place, upper = lax.rem(me, n // 2), me // (n // 2)
    row = lax.broadcasted_iota(jnp.int32, (2 * rows, tokens), 0)
    token = jnp.where(row < rows, place * rows + row, (place + n // 2) * rows + row - rows)
    own = token == lax.broadcasted_iota(jnp.int32, (2 * rows, tokens), 1)
    mask = jnp.sum(jnp.where(own, token_mask[...].astype(wide), 0.0), axis=1, keepdims=True)
    held[...] = mask * (one[...] + other[...].astype(wide) + dec_bias[...] - acts[place].astype(wide))
    copies[...] = jnp.broadcast_to(held[...].astype(half)[None], copies.shape)
    found = held[pl.ds(pl.multiple_of(upper * rows, rows), rows), :]
    error[...] = found
    means = jnp.mean(found * found, axis=1, keepdims=True)
    one = lax.broadcasted_iota(jnp.int32, (rows, rows), 0) == lax.broadcasted_iota(jnp.int32, (rows, rows), 1)
    squared[...] = jnp.sum(jnp.where(one, means, 0.0), axis=0, keepdims=True)


def finish(terms, error, squared, total, out, squared_out, total_out, held, done):
    moves = [(total, total_out), (squared, squared_out), (held, out)]
    moves = [pltpu.make_async_copy(here, there, done.at[i]) for i, (here, there) in enumerate(moves)]
    moves[0].start()
    moves[1].start()
    held[...] = (jnp.sum(terms[...].astype(wide), axis=0) - error[...]).astype(half)
    moves[2].start()
    for move in moves:
        move.wait()


def shards(activations, enc_weight, dec_weight, enc_bias, threshold, dec_bias, token_mask):
    n_feat = lax.axis_size("feat")
    tok_dev, _, depth = activations.shape
    tokens, width = n_feat * tok_dev, enc_bias.shape[0]
    enc, dec = enc_weight[0], dec_weight[0]
    acts = activations[:, 0]
    exchange = functools.partial(lax.all_to_all, axis_name="feat", split_axis=0, concat_axis=0)
    by_owner = (n_feat, tok_dev, depth)

    mirror = [(i, (i + n_feat // 2) % n_feat) for i in range(n_feat)]
    halves = [list(range(n_feat // 2)), list(range(n_feat // 2, n_feat))]
    by_pair = (n_feat // 2, 2 * tok_dev, depth)
    other = lax.ppermute(acts, "feat", mirror)
    [acts] = call(
        bring, [near(acts.shape, half)], acts, scratch=[pltpu.SemaphoreType.DMA], fetched=1, work=True
    )
    [copies] = call(join, [near(by_pair, half)], acts, other)
    [copies] = call(lambda *refs: None, [near(by_pair, half)], enc, dec, copies, fetched=2, same={2: 0})
    whole_acts = exchange(copies, axis_index_groups=halves)
    terms, enc_bias, threshold = call(
        functools.partial(encode_first, tok_dev),
        [near((tokens, width), half), near((1, width), wide), near((1, width), wide)],
        enc_bias[None],
        threshold[None],
        whole_acts,
        enc,
        scratch=[pltpu.SemaphoreType.DMA((2,))],
        fetched=2,
    )
    terms, others, dec_turned = swap_sums(terms, "layer", dec)
    decoded, slope = call(
        functools.partial(decode, tok_dev),
        [near((tokens, depth), half), near((tokens, width), wide)],
        terms,
        others,
        enc_bias,
        threshold,
        dec,
        dec_turned,
    )
    pieces = exchange(decoded.reshape(by_pair), axis_index_groups=halves)
    one, other = call(add_up, [near(by_pair[1:], wide), near(by_pair[1:], half)], pieces)
    other = lax.ppermute(other, "feat", mirror)
    error, copies, squared = call(
        compare,
        [near((tok_dev, depth), wide), near(by_pair, half), near((1, tok_dev), wide)],
        one,
        other,
        dec_bias,
        whole_acts,
        token_mask[None],
        scratch=[pltpu.VMEM(by_pair[1:], wide)],
    )
    error_all = exchange(copies, axis_index_groups=halves)
    [terms] = call(
        functools.partial(encode_paired, tok_dev), [near((tokens, width), half)], error_all, dec_turned
    )
    terms, others, enc_turned = swap_sums(terms, "layer", enc)
    grads, latent_grad = call(
        decode_grad,
        [near((tokens, depth), half), near((tokens, width), wide)],
        terms,
        others,
        slope,
        enc_turned,
    )
    pieces = exchange(grads.reshape(by_owner))
    input_grad, squared, latent_grad = call(
        finish,
        [free((tok_dev, depth), half), free((1, tok_dev), wide), free((tokens, width), wide)],
        pieces,
        error,
        squared,
        latent_grad,
        scratch=[pltpu.VMEM((tok_dev, depth), half), pltpu.SemaphoreType.DMA((3,))],
        sent=3,
    )
    return (squared.T, latent_grad, input_grad[:, None])


def solution(mesh):
    return jax.shard_map(
        shards,
        mesh=mesh,
        in_specs=(
            P("feat", "layer", None),
            P("layer", None, "feat"),
            P("layer", "feat", None),
            P("feat"),
            P("feat"),
            P("layer", None),
            P(),
        ),
        out_specs=(P("feat", "layer"), P(None, "feat"), P("feat", "layer", None)),
        check_vma=False,
    )
```

```python
import functools

import jax
import jax.numpy as jnp
from jax import lax
from jax.experimental import pallas as pl
from jax.experimental.pallas import tpu as pltpu
from jax.sharding import PartitionSpec as P


jump_scale = 0.25
columns = 256
half, wide = jnp.bfloat16, jnp.float32


def near(shape, dtype):
    return pltpu.VMEM(shape, dtype)


def free(shape, dtype):
    return jax.ShapeDtypeStruct(shape, dtype)


def call(body, outs, *args, scratch=(), fetched=0, sent=0, work=False, same={}):
    here, away = pl.BlockSpec(memory_space=pltpu.VMEM), pl.BlockSpec(memory_space=pl.ANY)
    size = sum(a.size * a.dtype.itemsize for a in args)
    cost = pl.CostEstimate(flops=0, transcendentals=0, bytes_accessed=2 * size) if work else None
    spaces = [pltpu.HBM] * fetched + [pltpu.VMEM] * (len(args) - fetched)
    return pl.pallas_call(
        body,
        out_shape=outs,
        in_specs=[away] * fetched + [here] * (len(args) - fetched),
        out_specs=[here] * (len(outs) - sent) + [away] * sent,
        scratch_shapes=scratch,
        compiler_params=pltpu.CompilerParams(vmem_limit_bytes=16 << 20),
        cost_estimate=cost,
        input_output_aliases=same,
    )(*map(pltpu.with_memory_space_constraint, args, spaces))


def swap_sums(terms, axis, weight):
    n, span = lax.axis_size(axis), 1
    while True:
        other = lax.ppermute(terms, axis, [(i, i ^ span) for i in range(n)])
        span *= 2
        if span == n:
            [turned] = call(turn, [near(weight.shape[::-1], half)], weight, terms, work=True)
            return terms, other, turned
        [terms] = call(add, [near(terms.shape, half)], terms, other)


def trade(pieces):
    n, came = lax.axis_size("feat"), list(pieces)
    for k in reversed(range(1, n // 2)):
        came[k] = lax.ppermute(pieces[k], "feat", [(i, i ^ k) for i in range(n)])
    return came


def mirror(block):
    n = lax.axis_size("feat")
    return lax.ppermute(block, "feat", [(i, (i + n // 2) % n) for i in range(n)])


def in_first_half():
    return lax.axis_index("feat") < lax.axis_size("feat") // 2


def place():
    return lax.rem(lax.axis_index("feat"), lax.axis_size("feat") // 2)


def stack(refs):
    return jnp.concatenate([ref[...] for ref in refs])


def sum_of(refs):
    return functools.reduce(lambda so_far, ref: so_far + ref[...].astype(wide), refs[1:], refs[0][...].astype(wide))


def own_and_mirror(pair):
    rows = pair.shape[0] // 2
    first, low, high = in_first_half(), pair[:rows], pair[rows:]
    return jnp.where(first, low, high), jnp.where(first, high, low)


def add(one, other, out):
    out[...] = (one[...].astype(wide) + other[...].astype(wide)).astype(half)


def bring(far, out, done):
    move = pltpu.make_async_copy(far, out, done)
    move.start()
    move.wait()


def join(acts, other, pair):
    first = in_first_half()
    mine, theirs = acts[...].astype(wide), other[...].astype(wide)
    both = [jnp.where(first, mine, theirs), jnp.where(first, theirs, mine)]
    pair[...] = jnp.concatenate(both).astype(half)


def encode(weight, *rest):
    *groups, out = rest
    x = stack(groups)
    for at in range(0, out.shape[1], columns):
        out[:, at : at + columns] = jnp.dot(
            x, weight[:, at : at + columns], preferred_element_type=wide
        ).astype(half)


def encode_first(enc_bias, threshold, weight, *rest):
    *rest, bias_near, threshold_near, done = rest
    moves = [
        pltpu.make_async_copy(enc_bias, bias_near, done.at[0]),
        pltpu.make_async_copy(threshold, threshold_near, done.at[1]),
    ]
    for move in moves:
        move.start()
    encode(weight, *rest)
    for move in moves:
        move.wait()


def turn(weight, after, out):
    for at in range(0, weight.shape[0], columns):
        out[:, at : at + columns] = weight[at : at + columns, :].T


def spread_rows(x, weight, outs):
    for at in range(0, weight.shape[1], columns):
        found = jnp.dot(x, weight[:, at : at + columns], preferred_element_type=wide).astype(half)
        for k, out in enumerate(outs):
            rows = out.shape[0]
            out[:, at : at + columns] = found[k * rows : (k + 1) * rows]


def decode(terms, others, enc_bias, threshold, weight, before, slope, *outs):
    preact = terms[...].astype(wide) + others[...].astype(wide) + enc_bias[...]
    gating = jax.nn.sigmoid((preact - threshold[...]) / jump_scale)
    slope[...] = gating + preact * gating * (1.0 - gating) / jump_scale
    spread_rows((preact * gating).astype(half), weight, outs)


def decode_grad(terms, others, slope, weight, total, *outs):
    latent_grad = terms[...].astype(wide) + others[...].astype(wide)
    n, me = 2 * len(outs), place()
    rows = total.shape[0] // n
    for i in range(n):
        block = lax.bitwise_xor(me, i // 2) + i % 2 * (n // 2)
        total[pl.ds(pl.multiple_of(block * rows, rows), rows), :] = latent_grad[i * rows : (i + 1) * rows]
    spread_rows((latent_grad * slope[...]).astype(half), weight, outs)


def add_pair(*refs):
    *terms, out, sent = refs
    found = sum_of(terms)
    out[...] = found
    sent[...] = found.astype(half)


def add_last(*refs):
    *terms, out, sent = refs
    mine, theirs = own_and_mirror(sum_of(terms))
    out[...] = mine
    sent[...] = theirs.astype(half)


def compare(one, other, dec_bias, acts, token_mask, error, pair, squared):
    rows, tokens = error.shape[0], token_mask.shape[1]
    row = lax.broadcasted_iota(jnp.int32, (2 * rows, tokens), 0)
    token = place() * rows + jnp.where(row < rows, row, tokens // 2 + row - rows)
    own = token == lax.broadcasted_iota(jnp.int32, (2 * rows, tokens), 1)
    mask = jnp.sum(jnp.where(own, token_mask[...].astype(wide), 0.0), axis=1, keepdims=True)
    both = mask * (one[...] + other[...].astype(wide) + dec_bias[...] - acts[...].astype(wide))
    pair[...] = both.astype(half)
    found, _ = own_and_mirror(both)
    error[...] = found
    means = jnp.mean(found * found, axis=1, keepdims=True)
    same = lax.broadcasted_iota(jnp.int32, (rows, rows), 0) == lax.broadcasted_iota(jnp.int32, (rows, rows), 1)
    squared[...] = jnp.sum(jnp.where(same, means, 0.0), axis=0, keepdims=True)


def finish(one, other, error, squared, grad, out, squared_out, grad_out, held, done):
    moves = [(grad, grad_out), (squared, squared_out), (held, out)]
    moves = [pltpu.make_async_copy(here, there, done.at[i]) for i, (here, there) in enumerate(moves)]
    moves[0].start()
    moves[1].start()
    held[...] = (one[...] + other[...].astype(wide) - error[...]).astype(half)
    moves[2].start()
    for move in moves:
        move.wait()


def shards(activations, enc_weight, dec_weight, enc_bias, threshold, dec_bias, token_mask):
    n_feat = lax.axis_size("feat")
    tok_dev, _, depth = activations.shape
    tokens, width, groups = n_feat * tok_dev, enc_bias.shape[0], n_feat // 2
    enc, dec = enc_weight[0], dec_weight[0]
    acts = activations[:, 0]
    own, pair = (tok_dev, depth), (2 * tok_dev, depth)

    other = mirror(acts)
    [acts] = call(bring, [near(own, half)], acts, scratch=[pltpu.SemaphoreType.DMA], fetched=1, work=True)
    [acts_pair] = call(join, [near(pair, half)], acts, other)
    [acts_pair] = call(lambda *refs: None, [near(pair, half)], enc, dec, acts_pair, fetched=2, same={2: 0})
    terms, enc_bias, threshold = call(
        encode_first,
        [near((tokens, width), half), near((1, width), wide), near((1, width), wide)],
        enc_bias[None],
        threshold[None],
        enc,
        *trade([acts_pair] * groups),
        scratch=[pltpu.SemaphoreType.DMA((2,))],
        fetched=2,
    )
    terms, others, dec_turned = swap_sums(terms, "layer", dec)
    slope, *decoded = call(
        decode,
        [near((tokens, width), wide)] + [near(pair, half)] * groups,
        terms,
        others,
        enc_bias,
        threshold,
        dec,
        dec_turned,
    )
    one, other = call(add_pair, [near(pair, wide), near(pair, half)], *trade(decoded))
    error, error_pair, squared = call(
        compare,
        [near(own, wide), near(pair, half), near((1, tok_dev), wide)],
        one,
        mirror(other),
        dec_bias,
        acts_pair,
        token_mask[None],
    )
    [terms] = call(encode, [near((tokens, width), half)], dec_turned, *trade([error_pair] * groups))
    terms, others, enc_turned = swap_sums(terms, "layer", enc)
    latent_grad, *grads = call(
        decode_grad,
        [near((tokens, width), wide)] + [near(pair, half)] * groups,
        terms,
        others,
        slope,
        enc_turned,
    )
    one, other = call(add_last, [near(own, wide), near(own, half)], *trade(grads))
    input_grad, squared, latent_grad = call(
        finish,
        [free(own, half), free((1, tok_dev), wide), free((tokens, width), wide)],
        one,
        mirror(other),
        error,
        squared,
        latent_grad,
        scratch=[pltpu.VMEM(own, half), pltpu.SemaphoreType.DMA((3,))],
        sent=3,
    )
    return (squared.T, latent_grad, input_grad[:, None])


def solution(mesh):
    return jax.shard_map(
        shards,
        mesh=mesh,
        in_specs=(
            P("feat", "layer", None),
            P("layer", None, "feat"),
            P("layer", "feat", None),
            P("feat"),
            P("feat"),
            P("layer", None),
            P(),
        ),
        out_specs=(P("feat", "layer"), P(None, "feat"), P("feat", "layer", None)),
        check_vma=False,
    )
```

```python
import functools

import jax
import jax.numpy as jnp
from jax import lax
from jax.experimental import pallas as pl
from jax.experimental.pallas import tpu as pltpu
from jax.sharding import PartitionSpec as P


jump_scale = 0.25
columns = 256
half, wide = jnp.bfloat16, jnp.float32


def near(shape, dtype):
    return pltpu.VMEM(shape, dtype)


def free(shape, dtype):
    return jax.ShapeDtypeStruct(shape, dtype)


def call(body, outs, *args, scratch=(), fetched=0, sent=0, work=False, same={}):
    here, away = pl.BlockSpec(memory_space=pltpu.VMEM), pl.BlockSpec(memory_space=pl.ANY)
    size = sum(a.size * a.dtype.itemsize for a in args)
    cost = pl.CostEstimate(flops=0, transcendentals=0, bytes_accessed=2 * size) if work else None
    spaces = [pltpu.HBM] * fetched + [pltpu.VMEM] * (len(args) - fetched)
    return pl.pallas_call(
        body,
        out_shape=outs,
        in_specs=[away] * fetched + [here] * (len(args) - fetched),
        out_specs=[here] * (len(outs) - sent) + [away] * sent,
        scratch_shapes=scratch,
        compiler_params=pltpu.CompilerParams(vmem_limit_bytes=16 << 20),
        cost_estimate=cost,
        input_output_aliases=same,
    )(*map(pltpu.with_memory_space_constraint, args, spaces))


def swap_sums(terms, axis, weight):
    n, span = lax.axis_size(axis), 1
    while True:
        other = lax.ppermute(terms, axis, [(i, i ^ span) for i in range(n)])
        span *= 2
        if span == n:
            [turned] = call(turn, [near(weight.shape[::-1], half)], weight, terms, work=True)
            return terms, other, turned
        [terms] = call(add, [near(terms.shape, half)], terms, other)


def trade(pieces):
    n, came = lax.axis_size("feat"), list(pieces)
    for k in reversed(range(1, n // 2)):
        came[k] = lax.ppermute(pieces[k], "feat", [(i, i ^ k) for i in range(n)])
    return came


def mirror(block):
    n = lax.axis_size("feat")
    return lax.ppermute(block, "feat", [(i, (i + n // 2) % n) for i in range(n)])


def in_first_half():
    return lax.axis_index("feat") < lax.axis_size("feat") // 2


def place():
    return lax.rem(lax.axis_index("feat"), lax.axis_size("feat") // 2)


def stack(refs):
    return jnp.concatenate([ref[...] for ref in refs])


def sum_of(refs):
    return functools.reduce(lambda so_far, ref: so_far + ref[...].astype(wide), refs[1:], refs[0][...].astype(wide))


def own_and_mirror(pair):
    rows = pair.shape[0] // 2
    first, low, high = in_first_half(), pair[:rows], pair[rows:]
    return jnp.where(first, low, high), jnp.where(first, high, low)


def add(one, other, out):
    out[...] = (one[...].astype(wide) + other[...].astype(wide)).astype(half)


def bring(far, out, done):
    move = pltpu.make_async_copy(far, out, done)
    move.start()
    move.wait()


def join(acts, other, pair):
    first = in_first_half()
    mine, theirs = acts[...].astype(wide), other[...].astype(wide)
    both = [jnp.where(first, mine, theirs), jnp.where(first, theirs, mine)]
    pair[...] = jnp.concatenate(both).astype(half)


def encode(weight, *rest):
    *groups, out = rest
    x = stack(groups)
    for at in range(0, out.shape[1], columns):
        out[:, at : at + columns] = jnp.dot(
            x, weight[:, at : at + columns], preferred_element_type=wide
        ).astype(half)


def encode_first(enc_bias, threshold, weight, *rest):
    *rest, bias_near, threshold_near, done = rest
    moves = [
        pltpu.make_async_copy(enc_bias, bias_near, done.at[0]),
        pltpu.make_async_copy(threshold, threshold_near, done.at[1]),
    ]
    for move in moves:
        move.start()
    encode(weight, *rest)
    for move in moves:
        move.wait()


def turn(weight, after, out):
    for at in range(0, weight.shape[0], columns):
        out[:, at : at + columns] = weight[at : at + columns, :].T


def spread_rows(x, weight, outs):
    for at in range(0, weight.shape[1], columns):
        found = jnp.dot(x, weight[:, at : at + columns], preferred_element_type=wide).astype(half)
        for k, out in enumerate(outs):
            rows = out.shape[0]
            out[:, at : at + columns] = found[k * rows : (k + 1) * rows]


def decode(terms, others, enc_bias, threshold, weight, before, slope, *outs):
    preact = terms[...].astype(wide) + others[...].astype(wide) + enc_bias[...]
    gating = jax.nn.sigmoid((preact - threshold[...]) / jump_scale)
    slope[...] = gating + preact * gating * (1.0 - gating) / jump_scale
    spread_rows((preact * gating).astype(half), weight, outs)


def decode_grad(terms, others, slope, weight, total, *outs):
    latent_grad = terms[...].astype(wide) + others[...].astype(wide)
    n, me = 2 * len(outs), place()
    rows = total.shape[0] // n
    for i in range(n):
        block = lax.bitwise_xor(me, i // 2) + i % 2 * (n // 2)
        total[pl.ds(pl.multiple_of(block * rows, rows), rows), :] = latent_grad[i * rows : (i + 1) * rows]
    spread_rows((latent_grad * slope[...]).astype(half), weight, outs)


def add_pair(*refs):
    *terms, out, sent = refs
    found = sum_of(terms)
    out[...] = found
    sent[...] = found.astype(half)


def add_last(*refs):
    *terms, out, sent = refs
    mine, theirs = own_and_mirror(sum_of(terms))
    out[...] = mine
    sent[...] = theirs.astype(half)


def compare(one, other, dec_bias, acts, token_mask, error, pair, squared):
    rows, tokens = error.shape[0], token_mask.shape[1]
    row = lax.broadcasted_iota(jnp.int32, (2 * rows, tokens), 0)
    token = place() * rows + jnp.where(row < rows, row, tokens // 2 + row - rows)
    own = token == lax.broadcasted_iota(jnp.int32, (2 * rows, tokens), 1)
    mask = jnp.sum(jnp.where(own, token_mask[...].astype(wide), 0.0), axis=1, keepdims=True)
    both = mask * (one[...] + other[...].astype(wide) + dec_bias[...] - acts[...].astype(wide))
    pair[...] = both.astype(half)
    found, _ = own_and_mirror(both)
    error[...] = found
    means = jnp.mean(found * found, axis=1, keepdims=True)
    same = lax.broadcasted_iota(jnp.int32, (rows, rows), 0) == lax.broadcasted_iota(jnp.int32, (rows, rows), 1)
    squared[...] = jnp.sum(jnp.where(same, means, 0.0), axis=0, keepdims=True)


def finish(one, other, error, squared, grad, out, squared_out, grad_out, held, done):
    moves = [(grad, grad_out), (squared, squared_out), (held, out)]
    moves = [pltpu.make_async_copy(here, there, done.at[i]) for i, (here, there) in enumerate(moves)]
    moves[0].start()
    moves[1].start()
    held[...] = (one[...] + other[...].astype(wide) - error[...]).astype(half)
    moves[2].start()
    for move in moves:
        move.wait()


def shards(activations, enc_weight, dec_weight, enc_bias, threshold, dec_bias, token_mask):
    n_feat = lax.axis_size("feat")
    tok_dev, _, depth = activations.shape
    tokens, width, groups = n_feat * tok_dev, enc_bias.shape[0], n_feat // 2
    enc, dec = enc_weight[0], dec_weight[0]
    acts = activations[:, 0]
    own, pair = (tok_dev, depth), (2 * tok_dev, depth)

    other = mirror(acts)
    [acts] = call(bring, [near(own, half)], acts, scratch=[pltpu.SemaphoreType.DMA], fetched=1, work=True)
    [acts_pair] = call(join, [near(pair, half)], acts, other)
    [acts_pair] = call(lambda *refs: None, [near(pair, half)], enc, dec, acts_pair, fetched=2, same={2: 0})
    terms, enc_bias, threshold = call(
        encode_first,
        [near((tokens, width), half), near((1, width), wide), near((1, width), wide)],
        enc_bias[None],
        threshold[None],
        enc,
        *trade([acts_pair] * groups),
        scratch=[pltpu.SemaphoreType.DMA((2,))],
        fetched=2,
    )
    terms, others, dec_turned = swap_sums(terms, "layer", dec)
    slope, *decoded = call(
        decode,
        [near((tokens, width), wide)] + [near(pair, half)] * groups,
        terms,
        others,
        enc_bias,
        threshold,
        dec,
        dec_turned,
    )
    one, other = call(add_pair, [near(pair, wide), near(pair, half)], *reversed(trade(decoded)))
    error, error_pair, squared = call(
        compare,
        [near(own, wide), near(pair, half), near((1, tok_dev), wide)],
        one,
        mirror(other),
        dec_bias,
        acts_pair,
        token_mask[None],
    )
    [terms] = call(encode, [near((tokens, width), half)], dec_turned, *trade([error_pair] * groups))
    terms, others, enc_turned = swap_sums(terms, "layer", enc)
    latent_grad, *grads = call(
        decode_grad,
        [near((tokens, width), wide)] + [near(pair, half)] * groups,
        terms,
        others,
        slope,
        enc_turned,
    )
    one, other = call(add_last, [near(own, wide), near(own, half)], *reversed(trade(grads)))
    input_grad, squared, latent_grad = call(
        finish,
        [free(own, half), free((1, tok_dev), wide), free((tokens, width), wide)],
        one,
        mirror(other),
        error,
        squared,
        latent_grad,
        scratch=[pltpu.VMEM(own, half), pltpu.SemaphoreType.DMA((3,))],
        sent=3,
    )
    return (squared.T, latent_grad, input_grad[:, None])


def solution(mesh):
    return jax.shard_map(
        shards,
        mesh=mesh,
        in_specs=(
            P("feat", "layer", None),
            P("layer", None, "feat"),
            P("layer", "feat", None),
            P("feat"),
            P("feat"),
            P("layer", None),
            P(),
        ),
        out_specs=(P("feat", "layer"), P(None, "feat"), P("feat", "layer", None)),
        check_vma=False,
    )
```

```python
import functools

import jax
import jax.numpy as jnp
from jax import lax
from jax.experimental import pallas as pl
from jax.experimental.pallas import tpu as pltpu
from jax.sharding import PartitionSpec as P


jump_scale = 0.25
columns = 256
half, wide = jnp.bfloat16, jnp.float32


def near(shape, dtype):
    return pltpu.VMEM(shape, dtype)


def free(shape, dtype):
    return jax.ShapeDtypeStruct(shape, dtype)


def call(body, outs, *args, scratch=(), fetched=0, sent=0, work=False, same={}):
    here, away = pl.BlockSpec(memory_space=pltpu.VMEM), pl.BlockSpec(memory_space=pl.ANY)
    size = sum(a.size * a.dtype.itemsize for a in args)
    cost = pl.CostEstimate(flops=0, transcendentals=0, bytes_accessed=2 * size) if work else None
    spaces = [pltpu.HBM] * fetched + [pltpu.VMEM] * (len(args) - fetched)
    return pl.pallas_call(
        body,
        out_shape=outs,
        in_specs=[away] * fetched + [here] * (len(args) - fetched),
        out_specs=[here] * (len(outs) - sent) + [away] * sent,
        scratch_shapes=scratch,
        compiler_params=pltpu.CompilerParams(vmem_limit_bytes=16 << 20),
        cost_estimate=cost,
        input_output_aliases=same,
    )(*map(pltpu.with_memory_space_constraint, args, spaces))


def layer_sum(make, weight):
    n = lax.axis_size("layer")
    near_by, far_off = [[(i, i ^ span) for i in range(n)] for span in (1, n // 2)]
    theirs = lax.ppermute(make(True), "layer", near_by)
    mine = make(False)
    [pair] = call(add, [near(mine.shape, half)], mine, theirs)
    [turned] = call(turn, [near(weight.shape[::-1], half)], weight, pair, work=True)
    far = lax.ppermute(pair, "layer", far_off)
    [far] = call(lambda *refs: None, [near(far.shape, half)], turned, far, same={1: 0})
    other = [lax.ppermute(x, "layer", near_by) for x in (pair, far)]
    return (pair, far), other, turned


def features(other, width):
    which = lax.rem(lax.axis_index("layer") + int(other), 2)
    return pl.ds(pl.multiple_of(which * width, width), width)


def trade(pieces):
    n, came = lax.axis_size("feat"), list(pieces)
    for k in reversed(range(1, n // 2)):
        came[k] = lax.ppermute(pieces[k], "feat", [(i, i ^ k) for i in range(n)])
    return came


def mirror(block):
    n = lax.axis_size("feat")
    return lax.ppermute(block, "feat", [(i, (i + n // 2) % n) for i in range(n)])


def in_first_half():
    return lax.axis_index("feat") < lax.axis_size("feat") // 2


def place():
    return lax.rem(lax.axis_index("feat"), lax.axis_size("feat") // 2)


def stack(refs):
    return jnp.concatenate([ref[...] for ref in refs])


def sum_of(refs):
    return functools.reduce(lambda so_far, ref: so_far + ref[...].astype(wide), refs[1:], refs[0][...].astype(wide))


def own_and_mirror(pair):
    rows = pair.shape[0] // 2
    first, low, high = in_first_half(), pair[:rows], pair[rows:]
    return jnp.where(first, low, high), jnp.where(first, high, low)


def add(one, other, out):
    out[...] = (one[...].astype(wide) + other[...].astype(wide)).astype(half)


def bring(*refs):
    *refs, done = refs
    n = len(refs) // 2
    moves = [pltpu.make_async_copy(refs[i], refs[n + i], done.at[i]) for i in range(n)]
    for move in moves:
        move.start()
    for move in moves:
        move.wait()


def join(acts, other, pair):
    first = in_first_half()
    mine, theirs = acts[...].astype(wide), other[...].astype(wide)
    both = [jnp.where(first, mine, theirs), jnp.where(first, theirs, mine)]
    pair[...] = jnp.concatenate(both).astype(half)


def encode(other, weight, *rest):
    *groups, out = rest
    x = stack(groups)
    first = features(other, out.shape[1]).start
    for at in range(0, out.shape[1], columns):
        there = pl.ds(pl.multiple_of(first + at, columns), columns)
        out[:, at : at + columns] = jnp.dot(x, weight[:, there], preferred_element_type=wide).astype(out.dtype)


def turn(weight, after, out):
    for at in range(0, weight.shape[0], columns):
        out[:, at : at + columns] = weight[at : at + columns, :].T


def spread_rows(x, weight, rows_in, so_far, outs):
    for at in range(0, weight.shape[1], columns):
        there = slice(at, at + columns)
        found = jnp.dot(x, weight[rows_in, there], preferred_element_type=wide)
        if so_far is None:
            outs[0][:, there] = found
            continue
        found = (found + so_far[:, there]).astype(half)
        for k, out in enumerate(outs):
            rows = out.shape[0]
            out[:, there] = found[k * rows : (k + 1) * rows]


def decode(other, terms, others, enc_bias, threshold, weight, before, slope, *outs):
    which = features(other, terms.shape[1])
    preact = terms[...].astype(wide) + others[...].astype(wide) + enc_bias[:, which]
    gating = jax.nn.sigmoid((preact - threshold[:, which]) / jump_scale)
    slope[...] = gating + preact * gating * (1.0 - gating) / jump_scale
    spread_rows((preact * gating).astype(half), weight, which, before if other else None, outs)


def decode_grad(other, terms, others, slope, weight, before, total, *outs):
    latent_grad = terms[...].astype(wide) + others[...].astype(wide)
    n, me = lax.axis_size("feat"), place()
    rows = total.shape[0] // n
    for i in range(n):
        block = lax.bitwise_xor(me, i // 2) + i % 2 * (n // 2)
        total[pl.ds(pl.multiple_of(block * rows, rows), rows), :] = latent_grad[i * rows : (i + 1) * rows]
    x = (latent_grad * slope[...]).astype(half)
    spread_rows(x, weight, features(other, terms.shape[1]), before if other else None, outs)


def add_pair(*refs):
    *terms, out, sent = refs
    found = sum_of(terms)
    out[...] = found
    sent[...] = found.astype(half)


def add_last(*refs):
    *terms, out, sent = refs
    mine, theirs = own_and_mirror(sum_of(terms))
    out[...] = mine
    sent[...] = theirs.astype(half)


def compare(one, other, dec_bias, acts, token_mask, error, pair, squared):
    rows, tokens = error.shape[0], token_mask.shape[1]
    row = lax.broadcasted_iota(jnp.int32, (2 * rows, tokens), 0)
    token = place() * rows + jnp.where(row < rows, row, tokens // 2 + row - rows)
    own = token == lax.broadcasted_iota(jnp.int32, (2 * rows, tokens), 1)
    mask = jnp.sum(jnp.where(own, token_mask[...].astype(wide), 0.0), axis=1, keepdims=True)
    both = mask * (one[...] + other[...].astype(wide) + dec_bias[...] - acts[...].astype(wide))
    pair[...] = both.astype(half)
    found, _ = own_and_mirror(both)
    error[...] = found
    means = jnp.mean(found * found, axis=1, keepdims=True)
    same = lax.broadcasted_iota(jnp.int32, (rows, rows), 0) == lax.broadcasted_iota(jnp.int32, (rows, rows), 1)
    squared[...] = jnp.sum(jnp.where(same, means, 0.0), axis=0, keepdims=True)


def finish(one, other, error, squared, grad, grad_other, out, squared_out, grad_out, held, done):
    mine, theirs = [grad_out.at[:, features(which, grad.shape[1])] for which in (False, True)]
    moves = [(grad, mine), (grad_other, theirs), (squared, squared_out), (held, out)]
    moves = [pltpu.make_async_copy(here, there, done.at[i]) for i, (here, there) in enumerate(moves)]
    for move in moves[:-1]:
        move.start()
    held[...] = (one[...] + other[...].astype(wide) - error[...]).astype(half)
    moves[-1].start()
    for move in moves:
        move.wait()


def shards(activations, enc_weight, dec_weight, enc_bias, threshold, dec_bias, token_mask):
    n_feat = lax.axis_size("feat")
    tok_dev, _, depth = activations.shape
    tokens, width, groups = n_feat * tok_dev, enc_bias.shape[0], n_feat // 2
    enc, dec = enc_weight[0], dec_weight[0]
    acts = activations[:, 0]
    own, pair = (tok_dev, depth), (2 * tok_dev, depth)

    other = mirror(acts)
    far = (acts, enc_bias[None], threshold[None])
    acts, enc_bias, threshold = call(
        bring,
        [near(x.shape, x.dtype) for x in far],
        *far,
        scratch=[pltpu.SemaphoreType.DMA((len(far),))],
        fetched=len(far),
        work=True,
    )
    [acts_pair] = call(join, [near(pair, half)], acts, other)
    [acts_pair] = call(lambda *refs: None, [near(pair, half)], enc, dec, acts_pair, fetched=2, same={2: 0})
    groups_of = trade([acts_pair] * groups)
    [sent] = call(functools.partial(encode, True), [near((tokens, width // 2), half)], enc, *groups_of)
    kept = lambda weight, given: call(
        functools.partial(encode, False), [near((tokens, width // 2), wide)], weight, *given
    )[0]
    mine, theirs, dec_turned = layer_sum(lambda other: sent if other else kept(enc, groups_of), dec)
    by_feature, whole = near((tokens, width // 2), wide), near((tokens, depth), wide)
    by_group = [near(pair, half)] * groups
    given = (enc_bias, threshold, dec)
    slope, part = call(functools.partial(decode, False), [by_feature, whole], *mine, *given, dec_turned)
    slope_other, *decoded = call(functools.partial(decode, True), [by_feature, *by_group], *theirs, *given, part)
    one, other = call(add_pair, [near(pair, wide), near(pair, half)], *reversed(trade(decoded)))
    error, error_pair, squared = call(
        compare,
        [near(own, wide), near(pair, half), near((1, tok_dev), wide)],
        one,
        mirror(other),
        dec_bias,
        acts_pair,
        token_mask[None],
    )
    errors = trade([error_pair] * groups)
    [sent] = call(functools.partial(encode, True), [near((tokens, width // 2), half)], dec_turned, *errors)
    mine, theirs, enc_turned = layer_sum(lambda other: sent if other else kept(dec_turned, errors), enc)
    grad, part = call(functools.partial(decode_grad, False), [by_feature, whole], *mine, slope, enc_turned, sent)
    grad_other, *grads = call(
        functools.partial(decode_grad, True), [by_feature, *by_group], *theirs, slope_other, enc_turned, part
    )
    one, other = call(add_last, [near(own, wide), near(own, half)], *reversed(trade(grads)))
    input_grad, squared, latent_grad = call(
        finish,
        [free(own, half), free((1, tok_dev), wide), free((tokens, width), wide)],
        one,
        mirror(other),
        error,
        squared,
        grad,
        grad_other,
        scratch=[pltpu.VMEM(own, half), pltpu.SemaphoreType.DMA((4,))],
        sent=3,
    )
    return (squared.T, latent_grad, input_grad[:, None])


def solution(mesh):
    return jax.shard_map(
        shards,
        mesh=mesh,
        in_specs=(
            P("feat", "layer", None),
            P("layer", None, "feat"),
            P("layer", "feat", None),
            P("feat"),
            P("feat"),
            P("layer", None),
            P(),
        ),
        out_specs=(P("feat", "layer"), P(None, "feat"), P("feat", "layer", None)),
        check_vma=False,
    )
```

```python
import functools

import jax
import jax.numpy as jnp
from jax import lax
from jax.experimental import pallas as pl
from jax.experimental.pallas import tpu as pltpu
from jax.sharding import PartitionSpec as P


jump_scale = 0.25
columns = 256
half, wide = jnp.bfloat16, jnp.float32


def near(shape, dtype):
    return pltpu.VMEM(shape, dtype)


def free(shape, dtype):
    return jax.ShapeDtypeStruct(shape, dtype)


def call(body, outs, *args, scratch=(), fetched=0, sent=0, work=False, same={}):
    here, away = pl.BlockSpec(memory_space=pltpu.VMEM), pl.BlockSpec(memory_space=pl.ANY)
    size = sum(a.size * a.dtype.itemsize for a in args)
    cost = pl.CostEstimate(flops=0, transcendentals=0, bytes_accessed=2 * size) if work else None
    spaces = [pltpu.HBM] * fetched + [pltpu.VMEM] * (len(args) - fetched)
    return pl.pallas_call(
        body,
        out_shape=outs,
        in_specs=[away] * fetched + [here] * (len(args) - fetched),
        out_specs=[here] * (len(outs) - sent) + [away] * sent,
        scratch_shapes=scratch,
        compiler_params=pltpu.CompilerParams(vmem_limit_bytes=16 << 20),
        cost_estimate=cost,
        input_output_aliases=same,
    )(*map(pltpu.with_memory_space_constraint, args, spaces))


def layer_sum(make, weight):
    n = lax.axis_size("layer")
    near_by, far_off = [[(i, i ^ span) for i in range(n)] for span in (1, n // 2)]
    theirs = lax.ppermute(make(True), "layer", near_by)
    mine = make(False)
    [pair] = call(add, [near(mine.shape, half)], mine, theirs)
    [turned] = call(turn, [near(weight.shape[::-1], half)], weight, pair, work=True)
    far = lax.ppermute(pair, "layer", far_off)
    [far] = call(lambda *refs: None, [near(far.shape, half)], turned, far, same={1: 0})
    other = [lax.ppermute(x, "layer", near_by) for x in (pair, far)]
    return (pair, far), other, turned


def features(other, width):
    which = lax.rem(lax.axis_index("layer") + int(other), 2)
    return pl.ds(pl.multiple_of(which * width, width), width)


def trade(pieces):
    n, came = lax.axis_size("feat"), list(pieces)
    for k in reversed(range(1, n // 2)):
        came[k] = lax.ppermute(pieces[k], "feat", [(i, i ^ k) for i in range(n)])
    return came


def mirror(block):
    n = lax.axis_size("feat")
    return lax.ppermute(block, "feat", [(i, (i + n // 2) % n) for i in range(n)])


def in_first_half():
    return lax.axis_index("feat") < lax.axis_size("feat") // 2


def place():
    return lax.rem(lax.axis_index("feat"), lax.axis_size("feat") // 2)


def last(came):
    return [*came[:2:-1], *came[1:3], came[0]]


def stack(refs):
    return jnp.concatenate([ref[...] for ref in refs])


def sum_of(refs):
    return functools.reduce(lambda so_far, ref: so_far + ref[...].astype(wide), refs[1:], refs[0][...].astype(wide))


def own_and_mirror(pair):
    rows = pair.shape[0] // 2
    first, low, high = in_first_half(), pair[:rows], pair[rows:]
    return jnp.where(first, low, high), jnp.where(first, high, low)


def add(one, other, out):
    out[...] = (one[...].astype(wide) + other[...].astype(wide)).astype(half)


def bring(*refs):
    *refs, done = refs
    n = len(refs) // 2
    moves = [pltpu.make_async_copy(refs[i], refs[n + i], done.at[i]) for i in range(n)]
    for move in moves:
        move.start()
    for move in moves:
        move.wait()


def join(acts, other, pair):
    first = in_first_half()
    mine, theirs = acts[...].astype(wide), other[...].astype(wide)
    both = [jnp.where(first, mine, theirs), jnp.where(first, theirs, mine)]
    pair[...] = jnp.concatenate(both).astype(half)


def encode(other, weight, *rest):
    *groups, out = rest
    x = stack(groups)
    first = features(other, out.shape[1]).start
    for at in range(0, out.shape[1], columns):
        there = pl.ds(pl.multiple_of(first + at, columns), columns)
        out[:, at : at + columns] = jnp.dot(x, weight[:, there], preferred_element_type=wide).astype(out.dtype)


def turn(weight, after, out):
    for at in range(0, weight.shape[0], columns):
        out[:, at : at + columns] = weight[at : at + columns, :].T


def spread_rows(x, weight, rows_in, so_far, outs):
    for at in range(0, weight.shape[1], columns):
        there = slice(at, at + columns)
        found = jnp.dot(x, weight[rows_in, there], preferred_element_type=wide)
        if so_far is None:
            outs[0][:, there] = found
            continue
        found = (found + so_far[:, there]).astype(half)
        for k, out in enumerate(outs):
            rows = out.shape[0]
            out[:, there] = found[k * rows : (k + 1) * rows]


def decode(other, terms, others, enc_bias, threshold, weight, before, slope, *outs):
    which = features(other, terms.shape[1])
    preact = terms[...].astype(wide) + others[...].astype(wide) + enc_bias[:, which]
    gating = jax.nn.sigmoid((preact - threshold[:, which]) / jump_scale)
    slope[...] = gating + preact * gating * (1.0 - gating) / jump_scale
    spread_rows((preact * gating).astype(half), weight, which, before if other else None, outs)


def decode_grad(other, terms, others, slope, weight, before, total, *outs):
    latent_grad = terms[...].astype(wide) + others[...].astype(wide)
    n, me = lax.axis_size("feat"), place()
    rows = total.shape[0] // n
    for i in range(n):
        block = lax.bitwise_xor(me, i // 2) + i % 2 * (n // 2)
        total[pl.ds(pl.multiple_of(block * rows, rows), rows), :] = latent_grad[i * rows : (i + 1) * rows]
    x = (latent_grad * slope[...]).astype(half)
    spread_rows(x, weight, features(other, terms.shape[1]), before if other else None, outs)


def add_pair(*refs):
    *terms, out, sent = refs
    found = sum_of(terms)
    out[...] = found
    sent[...] = found.astype(half)


def add_last(*refs):
    *terms, out, sent = refs
    mine, theirs = own_and_mirror(sum_of(terms))
    out[...] = mine
    sent[...] = theirs.astype(half)


def compare(one, other, dec_bias, acts, token_mask, error, pair, squared):
    rows, tokens = error.shape[0], token_mask.shape[1]
    row = lax.broadcasted_iota(jnp.int32, (2 * rows, tokens), 0)
    token = place() * rows + jnp.where(row < rows, row, tokens // 2 + row - rows)
    own = token == lax.broadcasted_iota(jnp.int32, (2 * rows, tokens), 1)
    mask = jnp.sum(jnp.where(own, token_mask[...].astype(wide), 0.0), axis=1, keepdims=True)
    both = mask * (one[...] + other[...].astype(wide) + dec_bias[...] - acts[...].astype(wide))
    pair[...] = both.astype(half)
    found, _ = own_and_mirror(both)
    error[...] = found
    means = jnp.mean(found * found, axis=1, keepdims=True)
    same = lax.broadcasted_iota(jnp.int32, (rows, rows), 0) == lax.broadcasted_iota(jnp.int32, (rows, rows), 1)
    squared[...] = jnp.sum(jnp.where(same, means, 0.0), axis=0, keepdims=True)


def leave(grad, grad_other, squared, grad_out, squared_out, done):
    mine, theirs = [grad_out.at[:, features(which, grad.shape[1])] for which in (False, True)]
    moves = [(grad, mine), (grad_other, theirs), (squared, squared_out)]
    moves = [pltpu.make_async_copy(here, there, done.at[i]) for i, (here, there) in enumerate(moves)]
    for move in moves:
        move.start()
    for move in moves:
        move.wait()


def finish(one, other, error, out):
    out[...] = (one[...] + other[...].astype(wide) - error[...]).astype(half)


def shards(activations, enc_weight, dec_weight, enc_bias, threshold, dec_bias, token_mask):
    n_feat = lax.axis_size("feat")
    tok_dev, _, depth = activations.shape
    tokens, width, groups = n_feat * tok_dev, enc_bias.shape[0], n_feat // 2
    enc, dec = enc_weight[0], dec_weight[0]
    acts = activations[:, 0]
    own, pair = (tok_dev, depth), (2 * tok_dev, depth)

    other = mirror(acts)
    far = (acts, enc_bias[None], threshold[None])
    acts, enc_bias, threshold = call(
        bring,
        [near(x.shape, x.dtype) for x in far],
        *far,
        scratch=[pltpu.SemaphoreType.DMA((len(far),))],
        fetched=len(far),
        work=True,
    )
    [acts_pair] = call(join, [near(pair, half)], acts, other)
    [acts_pair] = call(lambda *refs: None, [near(pair, half)], enc, dec, acts_pair, fetched=2, same={2: 0})
    groups_of = trade([acts_pair] * groups)
    [sent] = call(functools.partial(encode, True), [near((tokens, width // 2), half)], enc, *groups_of)
    kept = lambda weight, given: call(
        functools.partial(encode, False), [near((tokens, width // 2), wide)], weight, *given
    )[0]
    mine, theirs, dec_turned = layer_sum(lambda other: sent if other else kept(enc, groups_of), dec)
    by_feature, whole = near((tokens, width // 2), wide), near((tokens, depth), wide)
    by_group = [near(pair, half)] * groups
    given = (enc_bias, threshold, dec)
    slope, part = call(functools.partial(decode, False), [by_feature, whole], *mine, *given, dec_turned)
    slope_other, *decoded = call(functools.partial(decode, True), [by_feature, *by_group], *theirs, *given, part)
    one, other = call(add_pair, [near(pair, wide), near(pair, half)], *reversed(trade(decoded)))
    error, error_pair, squared = call(
        compare,
        [near(own, wide), near(pair, half), near((1, tok_dev), wide)],
        one,
        mirror(other),
        dec_bias,
        acts_pair,
        token_mask[None],
    )
    errors = trade([error_pair] * groups)
    [sent] = call(functools.partial(encode, True), [near((tokens, width // 2), half)], dec_turned, *errors)
    mine, theirs, enc_turned = layer_sum(lambda other: sent if other else kept(dec_turned, errors), enc)
    grad, part = call(functools.partial(decode_grad, False), [by_feature, whole], *mine, slope, enc_turned, sent)
    grad_other, *grads = call(
        functools.partial(decode_grad, True), [by_feature, *by_group], *theirs, slope_other, enc_turned, part
    )
    one, other = call(add_last, [near(own, wide), near(own, half)], *last(trade(grads)))
    latent_grad, squared = call(
        leave,
        [free((tokens, width), wide), free((1, tok_dev), wide)],
        grad,
        grad_other,
        squared,
        scratch=[pltpu.SemaphoreType.DMA((3,))],
        sent=2,
        work=True,
    )
    [input_grad] = call(finish, [free(own, half)], one, mirror(other), error)
    return (squared.T, latent_grad, input_grad[:, None])


def solution(mesh):
    return jax.shard_map(
        shards,
        mesh=mesh,
        in_specs=(
            P("feat", "layer", None),
            P("layer", None, "feat"),
            P("layer", "feat", None),
            P("feat"),
            P("feat"),
            P("layer", None),
            P(),
        ),
        out_specs=(P("feat", "layer"), P(None, "feat"), P("feat", "layer", None)),
        check_vma=False,
    )
```

```python
import functools

import jax
import jax.numpy as jnp
from jax import lax
from jax.experimental import pallas as pl
from jax.experimental.pallas import tpu as pltpu
from jax.sharding import PartitionSpec as P


jump_scale = 0.25
columns = 256
half, wide = jnp.bfloat16, jnp.float32


def near(shape, dtype):
    return pltpu.VMEM(shape, dtype)


def free(shape, dtype):
    return jax.ShapeDtypeStruct(shape, dtype)


def call(body, outs, *args, scratch=(), fetched=0, sent=0, work=False, same={}):
    here, away = pl.BlockSpec(memory_space=pltpu.VMEM), pl.BlockSpec(memory_space=pl.ANY)
    size = sum(a.size * a.dtype.itemsize for a in args)
    cost = pl.CostEstimate(flops=0, transcendentals=0, bytes_accessed=2 * size) if work else None
    spaces = [pltpu.HBM] * fetched + [pltpu.VMEM] * (len(args) - fetched)
    return pl.pallas_call(
        body,
        out_shape=outs,
        in_specs=[away] * fetched + [here] * (len(args) - fetched),
        out_specs=[here] * (len(outs) - sent) + [away] * sent,
        scratch_shapes=scratch,
        compiler_params=pltpu.CompilerParams(vmem_limit_bytes=16 << 20),
        cost_estimate=cost,
        input_output_aliases=same,
    )(*map(pltpu.with_memory_space_constraint, args, spaces))


def layer_sum(make, weight):
    n = lax.axis_size("layer")
    near_by, far_off = [[(i, i ^ span) for i in range(n)] for span in (1, n // 2 + 1)]
    theirs = lax.ppermute(make(True), "layer", near_by)
    mine = make(False)
    [pair] = call(add, [near(mine.shape, half)], mine, theirs)
    [turned] = call(turn, [near(weight.shape[::-1], half)], weight, pair, work=True)
    far = lax.ppermute(pair, "layer", far_off)
    [far] = call(lambda *refs: None, [near(far.shape, half)], turned, far, same={1: 0})
    back = [lax.ppermute(x, "layer", near_by) for x in (pair, far)]
    return (back[0], far), (pair, back[1]), turned


def features(other, width):
    which = lax.rem(lax.axis_index("layer") + int(other), 2)
    return pl.ds(pl.multiple_of(which * width, width), width)


def trade(pieces):
    n, came = lax.axis_size("feat"), list(pieces)
    for k in reversed(range(1, n // 2)):
        came[k] = lax.ppermute(pieces[k], "feat", [(i, i ^ k) for i in range(n)])
    return came


def mirror(block):
    n = lax.axis_size("feat")
    return lax.ppermute(block, "feat", [(i, (i + n // 2) % n) for i in range(n)])


def in_first_half():
    return lax.axis_index("feat") < lax.axis_size("feat") // 2


def place():
    return lax.rem(lax.axis_index("feat"), lax.axis_size("feat") // 2)


def last(came):
    return [*came[:2:-1], *came[1:3], came[0]]


def stack(refs):
    return jnp.concatenate([ref[...] for ref in refs])


def sum_of(refs):
    return functools.reduce(lambda so_far, ref: so_far + ref[...].astype(wide), refs[1:], refs[0][...].astype(wide))


def own_and_mirror(pair):
    rows = pair.shape[0] // 2
    first, low, high = in_first_half(), pair[:rows], pair[rows:]
    return jnp.where(first, low, high), jnp.where(first, high, low)


def add(one, other, out):
    out[...] = (one[...].astype(wide) + other[...].astype(wide)).astype(half)


def bring(*refs):
    *refs, done = refs
    n = len(refs) // 2
    moves = [pltpu.make_async_copy(refs[i], refs[n + i], done.at[i]) for i in range(n)]
    for move in moves:
        move.start()
    for move in moves:
        move.wait()


def join(acts, other, pair):
    first = in_first_half()
    mine, theirs = acts[...].astype(wide), other[...].astype(wide)
    both = [jnp.where(first, mine, theirs), jnp.where(first, theirs, mine)]
    pair[...] = jnp.concatenate(both).astype(half)


def encode(other, weight, *rest):
    *groups, out = rest
    x = stack(groups)
    first = features(other, out.shape[1]).start
    for at in range(0, out.shape[1], columns):
        there = pl.ds(pl.multiple_of(first + at, columns), columns)
        out[:, at : at + columns] = jnp.dot(x, weight[:, there], preferred_element_type=wide).astype(out.dtype)


def turn(weight, after, out):
    for at in range(0, weight.shape[0], columns):
        out[:, at : at + columns] = weight[at : at + columns, :].T


def spread_rows(x, weight, rows_in, so_far, outs):
    for at in range(0, weight.shape[1], columns):
        there = slice(at, at + columns)
        found = jnp.dot(x, weight[rows_in, there], preferred_element_type=wide)
        if so_far is None:
            outs[0][:, there] = found
            continue
        found = (found + so_far[:, there]).astype(half)
        for k, out in enumerate(outs):
            rows = out.shape[0]
            out[:, there] = found[k * rows : (k + 1) * rows]


def decode(last, terms, others, enc_bias, threshold, weight, before, slope, *outs):
    which = features(not last, terms.shape[1])
    preact = terms[...].astype(wide) + others[...].astype(wide) + enc_bias[:, which]
    gating = jax.nn.sigmoid((preact - threshold[:, which]) / jump_scale)
    slope[...] = gating + preact * gating * (1.0 - gating) / jump_scale
    spread_rows((preact * gating).astype(half), weight, which, before if last else None, outs)


def decode_grad(last, terms, others, slope, weight, before, total, *outs):
    latent_grad = terms[...].astype(wide) + others[...].astype(wide)
    n, me = lax.axis_size("feat"), place()
    rows = total.shape[0] // n
    for i in range(n):
        block = lax.bitwise_xor(me, i // 2) + i % 2 * (n // 2)
        total[pl.ds(pl.multiple_of(block * rows, rows), rows), :] = latent_grad[i * rows : (i + 1) * rows]
    x = (latent_grad * slope[...]).astype(half)
    spread_rows(x, weight, features(not last, terms.shape[1]), before if last else None, outs)


def add_pair(*refs):
    *terms, out, sent = refs
    found = sum_of(terms)
    out[...] = found
    sent[...] = found.astype(half)


def add_last(*refs):
    *terms, out, sent = refs
    mine, theirs = own_and_mirror(sum_of(terms))
    out[...] = mine
    sent[...] = theirs.astype(half)


def compare(one, other, dec_bias, acts, token_mask, error, pair, squared):
    rows, tokens = error.shape[0], token_mask.shape[1]
    row = lax.broadcasted_iota(jnp.int32, (2 * rows, tokens), 0)
    token = place() * rows + jnp.where(row < rows, row, tokens // 2 + row - rows)
    own = token == lax.broadcasted_iota(jnp.int32, (2 * rows, tokens), 1)
    mask = jnp.sum(jnp.where(own, token_mask[...].astype(wide), 0.0), axis=1, keepdims=True)
    both = mask * (one[...] + other[...].astype(wide) + dec_bias[...] - acts[...].astype(wide))
    pair[...] = both.astype(half)
    found, _ = own_and_mirror(both)
    error[...] = found
    means = jnp.mean(found * found, axis=1, keepdims=True)
    same = lax.broadcasted_iota(jnp.int32, (rows, rows), 0) == lax.broadcasted_iota(jnp.int32, (rows, rows), 1)
    squared[...] = jnp.sum(jnp.where(same, means, 0.0), axis=0, keepdims=True)


def leave(grad, grad_other, squared, grad_out, squared_out, done):
    mine, theirs = [grad_out.at[:, features(which, grad.shape[1])] for which in (True, False)]
    moves = [(grad, mine), (grad_other, theirs), (squared, squared_out)]
    moves = [pltpu.make_async_copy(here, there, done.at[i]) for i, (here, there) in enumerate(moves)]
    for move in moves:
        move.start()
    for move in moves:
        move.wait()


def finish(one, other, error, out):
    out[...] = (one[...] + other[...].astype(wide) - error[...]).astype(half)


def shards(activations, enc_weight, dec_weight, enc_bias, threshold, dec_bias, token_mask):
    n_feat = lax.axis_size("feat")
    tok_dev, _, depth = activations.shape
    tokens, width, groups = n_feat * tok_dev, enc_bias.shape[0], n_feat // 2
    enc, dec = enc_weight[0], dec_weight[0]
    acts = activations[:, 0]
    own, pair = (tok_dev, depth), (2 * tok_dev, depth)

    other = mirror(acts)
    far = (acts, enc_bias[None], threshold[None])
    acts, enc_bias, threshold = call(
        bring,
        [near(x.shape, x.dtype) for x in far],
        *far,
        scratch=[pltpu.SemaphoreType.DMA((len(far),))],
        fetched=len(far),
        work=True,
    )
    [acts_pair] = call(join, [near(pair, half)], acts, other)
    [acts_pair] = call(lambda *refs: None, [near(pair, half)], enc, dec, acts_pair, fetched=2, same={2: 0})
    groups_of = trade([acts_pair] * groups)
    [sent] = call(functools.partial(encode, True), [near((tokens, width // 2), half)], enc, *groups_of)
    kept = lambda weight, given: call(
        functools.partial(encode, False), [near((tokens, width // 2), wide)], weight, *given
    )[0]
    mine, theirs, dec_turned = layer_sum(lambda other: sent if other else kept(enc, groups_of), dec)
    by_feature, whole = near((tokens, width // 2), wide), near((tokens, depth), wide)
    by_group = [near(pair, half)] * groups
    given = (enc_bias, threshold, dec)
    slope, part = call(functools.partial(decode, False), [by_feature, whole], *mine, *given, dec_turned)
    slope_other, *decoded = call(functools.partial(decode, True), [by_feature, *by_group], *theirs, *given, part)
    one, other = call(add_pair, [near(pair, wide), near(pair, half)], *reversed(trade(decoded)))
    error, error_pair, squared = call(
        compare,
        [near(own, wide), near(pair, half), near((1, tok_dev), wide)],
        one,
        mirror(other),
        dec_bias,
        acts_pair,
        token_mask[None],
    )
    errors = trade([error_pair] * groups)
    [sent] = call(functools.partial(encode, True), [near((tokens, width // 2), half)], dec_turned, *errors)
    mine, theirs, enc_turned = layer_sum(lambda other: sent if other else kept(dec_turned, errors), enc)
    grad, part = call(functools.partial(decode_grad, False), [by_feature, whole], *mine, slope, enc_turned, sent)
    grad_other, *grads = call(
        functools.partial(decode_grad, True), [by_feature, *by_group], *theirs, slope_other, enc_turned, part
    )
    one, other = call(add_last, [near(own, wide), near(own, half)], *last(trade(grads)))
    latent_grad, squared = call(
        leave,
        [free((tokens, width), wide), free((1, tok_dev), wide)],
        grad,
        grad_other,
        squared,
        scratch=[pltpu.SemaphoreType.DMA((3,))],
        sent=2,
        work=True,
    )
    [input_grad] = call(finish, [free(own, half)], one, mirror(other), error)
    return (squared.T, latent_grad, input_grad[:, None])


def solution(mesh):
    return jax.shard_map(
        shards,
        mesh=mesh,
        in_specs=(
            P("feat", "layer", None),
            P("layer", None, "feat"),
            P("layer", "feat", None),
            P("feat"),
            P("feat"),
            P("layer", None),
            P(),
        ),
        out_specs=(P("feat", "layer"), P(None, "feat"), P("feat", "layer", None)),
        check_vma=False,
    )
```

```python
import functools

import jax
import jax.numpy as jnp
from jax import lax
from jax.experimental import pallas as pl
from jax.experimental.pallas import tpu as pltpu
from jax.sharding import PartitionSpec as P


jump_scale = 0.25
columns = 256
half, wide = jnp.bfloat16, jnp.float32


def near(shape, dtype):
    return pltpu.VMEM(shape, dtype)


def free(shape, dtype):
    return jax.ShapeDtypeStruct(shape, dtype)


def call(body, outs, *args, scratch=(), fetched=0, sent=0, work=False, same={}):
    here, away = pl.BlockSpec(memory_space=pltpu.VMEM), pl.BlockSpec(memory_space=pl.ANY)
    size = sum(a.size * a.dtype.itemsize for a in args)
    cost = pl.CostEstimate(flops=0, transcendentals=0, bytes_accessed=2 * size) if work else None
    spaces = [pltpu.HBM] * fetched + [pltpu.VMEM] * (len(args) - fetched)
    return pl.pallas_call(
        body,
        out_shape=outs,
        in_specs=[away] * fetched + [here] * (len(args) - fetched),
        out_specs=[here] * (len(outs) - sent) + [away] * sent,
        scratch_shapes=scratch,
        compiler_params=pltpu.CompilerParams(vmem_limit_bytes=16 << 20),
        cost_estimate=cost,
        input_output_aliases=same,
    )(*map(pltpu.with_memory_space_constraint, args, spaces))


def layer_sum(make, weight):
    n = lax.axis_size("layer")
    near_by, far_off = [[(i, i ^ span) for i in range(n)] for span in (1, n // 2 + 1)]
    theirs = lax.ppermute(make(True), "layer", near_by)
    mine = make(False)
    [pair] = call(add, [near(mine.shape, half)], mine, theirs)
    [turned] = call(turn, [near(weight.shape[::-1], half)], weight, pair, work=True)
    far = lax.ppermute(pair, "layer", far_off)
    [far] = call(lambda *refs: None, [near(far.shape, half)], turned, far, same={1: 0})
    back = [lax.ppermute(x, "layer", near_by) for x in (pair, far)]
    return (back[0], far), (pair, back[1]), turned


def features(other, width):
    which = lax.rem(lax.axis_index("layer") + int(other), 2)
    return pl.ds(pl.multiple_of(which * width, width), width)


def trade(pieces):
    n, came = lax.axis_size("feat"), list(pieces)
    for k in reversed(range(1, n // 2)):
        came[k] = lax.ppermute(pieces[k], "feat", [(i, i ^ k) for i in range(n)])
    return came


def mirror(block):
    n = lax.axis_size("feat")
    return lax.ppermute(block, "feat", [(i, (i + n // 2) % n) for i in range(n)])


def in_first_half():
    return lax.axis_index("feat") < lax.axis_size("feat") // 2


def place():
    return lax.rem(lax.axis_index("feat"), lax.axis_size("feat") // 2)


def nearest_last(came):
    return [came[0], *came[:0:-1]]


def last(came):
    return [*came[:2:-1], *came[1:3], came[0]]


def stack(refs):
    return jnp.concatenate([ref[...] for ref in refs])


def sum_of(refs):
    return functools.reduce(lambda so_far, ref: so_far + ref[...].astype(wide), refs[1:], refs[0][...].astype(wide))


def own_and_mirror(pair):
    rows = pair.shape[0] // 2
    first, low, high = in_first_half(), pair[:rows], pair[rows:]
    return jnp.where(first, low, high), jnp.where(first, high, low)


def add(one, other, out):
    out[...] = (one[...].astype(wide) + other[...].astype(wide)).astype(half)


def bring(*refs):
    *refs, done = refs
    n = len(refs) // 2
    moves = [pltpu.make_async_copy(refs[i], refs[n + i], done.at[i]) for i in range(n)]
    for move in moves:
        move.start()
    for move in moves:
        move.wait()


def join(acts, other, pair):
    first = in_first_half()
    mine, theirs = acts[...].astype(wide), other[...].astype(wide)
    both = [jnp.where(first, mine, theirs), jnp.where(first, theirs, mine)]
    pair[...] = jnp.concatenate(both).astype(half)


def encode(other, weight, *rest):
    *groups, out = rest
    x = stack(groups)
    first = features(other, out.shape[1]).start
    for at in range(0, out.shape[1], columns):
        there = pl.ds(pl.multiple_of(first + at, columns), columns)
        out[:, at : at + columns] = jnp.dot(x, weight[:, there], preferred_element_type=wide).astype(out.dtype)


def turn(weight, after, out):
    for at in range(0, weight.shape[0], columns):
        out[:, at : at + columns] = weight[at : at + columns, :].T


def spread_rows(x, weight, rows_in, so_far, outs):
    for at in range(0, weight.shape[1], columns):
        there = slice(at, at + columns)
        found = jnp.dot(x, weight[rows_in, there], preferred_element_type=wide)
        if so_far is None:
            outs[0][:, there] = found
            continue
        found = (found + so_far[:, there]).astype(half)
        for k, out in enumerate(outs):
            rows = out.shape[0]
            out[:, there] = found[k * rows : (k + 1) * rows]


def decode(last, terms, others, enc_bias, threshold, weight, before, slope, *outs):
    which = features(not last, terms.shape[1])
    preact = terms[...].astype(wide) + others[...].astype(wide) + enc_bias[:, which]
    gating = jax.nn.sigmoid((preact - threshold[:, which]) / jump_scale)
    slope[...] = gating + preact * gating * (1.0 - gating) / jump_scale
    spread_rows((preact * gating).astype(half), weight, which, before if last else None, outs)


def decode_grad(last, terms, others, slope, weight, before, total, *outs):
    latent_grad = terms[...].astype(wide) + others[...].astype(wide)
    n, me = lax.axis_size("feat"), place()
    rows = total.shape[0] // n
    for i in range(n):
        block = lax.bitwise_xor(me, i // 2) + i % 2 * (n // 2)
        total[pl.ds(pl.multiple_of(block * rows, rows), rows), :] = latent_grad[i * rows : (i + 1) * rows]
    x = (latent_grad * slope[...]).astype(half)
    spread_rows(x, weight, features(not last, terms.shape[1]), before if last else None, outs)


def add_pair(*refs):
    *terms, out, sent = refs
    found = sum_of(terms)
    out[...] = found
    sent[...] = found.astype(half)


def add_last(*refs):
    *terms, out, sent = refs
    mine, theirs = own_and_mirror(sum_of(terms))
    out[...] = mine
    sent[...] = theirs.astype(half)


def compare(one, other, dec_bias, acts, token_mask, error, pair, squared):
    rows, tokens = error.shape[0], token_mask.shape[1]
    row = lax.broadcasted_iota(jnp.int32, (2 * rows, tokens), 0)
    token = place() * rows + jnp.where(row < rows, row, tokens // 2 + row - rows)
    own = token == lax.broadcasted_iota(jnp.int32, (2 * rows, tokens), 1)
    mask = jnp.sum(jnp.where(own, token_mask[...].astype(wide), 0.0), axis=1, keepdims=True)
    both = mask * (one[...] + other[...].astype(wide) + dec_bias[...] - acts[...].astype(wide))
    pair[...] = both.astype(half)
    found, _ = own_and_mirror(both)
    error[...] = found
    means = jnp.mean(found * found, axis=1, keepdims=True)
    same = lax.broadcasted_iota(jnp.int32, (rows, rows), 0) == lax.broadcasted_iota(jnp.int32, (rows, rows), 1)
    squared[...] = jnp.sum(jnp.where(same, means, 0.0), axis=0, keepdims=True)


def leave(grad, grad_other, squared, grad_out, squared_out, done):
    mine, theirs = [grad_out.at[:, features(which, grad.shape[1])] for which in (True, False)]
    moves = [(grad, mine), (grad_other, theirs), (squared, squared_out)]
    moves = [pltpu.make_async_copy(here, there, done.at[i]) for i, (here, there) in enumerate(moves)]
    for move in moves:
        move.start()
    for move in moves:
        move.wait()


def finish(one, other, error, out):
    out[...] = (one[...] + other[...].astype(wide) - error[...]).astype(half)


def shards(activations, enc_weight, dec_weight, enc_bias, threshold, dec_bias, token_mask):
    n_feat = lax.axis_size("feat")
    tok_dev, _, depth = activations.shape
    tokens, width, groups = n_feat * tok_dev, enc_bias.shape[0], n_feat // 2
    enc, dec = enc_weight[0], dec_weight[0]
    acts = activations[:, 0]
    own, pair = (tok_dev, depth), (2 * tok_dev, depth)

    other = mirror(acts)
    far = (acts, enc_bias[None], threshold[None])
    acts, enc_bias, threshold = call(
        bring,
        [near(x.shape, x.dtype) for x in far],
        *far,
        scratch=[pltpu.SemaphoreType.DMA((len(far),))],
        fetched=len(far),
        work=True,
    )
    [acts_pair] = call(join, [near(pair, half)], acts, other)
    [acts_pair] = call(lambda *refs: None, [near(pair, half)], enc, dec, acts_pair, fetched=2, same={2: 0})
    groups_of = trade([acts_pair] * groups)
    [sent] = call(functools.partial(encode, True), [near((tokens, width // 2), half)], enc, *groups_of)
    kept = lambda weight, given: call(
        functools.partial(encode, False), [near((tokens, width // 2), wide)], weight, *given
    )[0]
    mine, theirs, dec_turned = layer_sum(lambda other: sent if other else kept(enc, groups_of), dec)
    by_feature, whole = near((tokens, width // 2), wide), near((tokens, depth), wide)
    by_group = [near(pair, half)] * groups
    given = (enc_bias, threshold, dec)
    slope, part = call(functools.partial(decode, False), [by_feature, whole], *mine, *given, dec_turned)
    slope_other, *decoded = call(functools.partial(decode, True), [by_feature, *by_group], *theirs, *given, part)
    one, other = call(add_pair, [near(pair, wide), near(pair, half)], *nearest_last(trade(decoded)))
    error, error_pair, squared = call(
        compare,
        [near(own, wide), near(pair, half), near((1, tok_dev), wide)],
        one,
        mirror(other),
        dec_bias,
        acts_pair,
        token_mask[None],
    )
    errors = trade([error_pair] * groups)
    [sent] = call(functools.partial(encode, True), [near((tokens, width // 2), half)], dec_turned, *errors)
    mine, theirs, enc_turned = layer_sum(lambda other: sent if other else kept(dec_turned, errors), enc)
    grad, part = call(functools.partial(decode_grad, False), [by_feature, whole], *mine, slope, enc_turned, sent)
    grad_other, *grads = call(
        functools.partial(decode_grad, True), [by_feature, *by_group], *theirs, slope_other, enc_turned, part
    )
    one, other = call(add_last, [near(own, wide), near(own, half)], *last(trade(grads)))
    latent_grad, squared = call(
        leave,
        [free((tokens, width), wide), free((1, tok_dev), wide)],
        grad,
        grad_other,
        squared,
        scratch=[pltpu.SemaphoreType.DMA((3,))],
        sent=2,
        work=True,
    )
    [input_grad] = call(finish, [free(own, half)], one, mirror(other), error)
    return (squared.T, latent_grad, input_grad[:, None])


def solution(mesh):
    return jax.shard_map(
        shards,
        mesh=mesh,
        in_specs=(
            P("feat", "layer", None),
            P("layer", None, "feat"),
            P("layer", "feat", None),
            P("feat"),
            P("feat"),
            P("layer", None),
            P(),
        ),
        out_specs=(P("feat", "layer"), P(None, "feat"), P("feat", "layer", None)),
        check_vma=False,
    )
```

```python
import functools

import jax
import jax.numpy as jnp
from jax import lax
from jax.experimental import pallas as pl
from jax.experimental.pallas import tpu as pltpu
from jax.sharding import PartitionSpec as P


jump_scale = 0.25
columns = 256
half, wide = jnp.bfloat16, jnp.float32


def near(shape, dtype):
    return pltpu.VMEM(shape, dtype)


def free(shape, dtype):
    return jax.ShapeDtypeStruct(shape, dtype)


def call(body, outs, *args, scratch=(), fetched=0, sent=0, work=False, same={}):
    here, away = pl.BlockSpec(memory_space=pltpu.VMEM), pl.BlockSpec(memory_space=pl.ANY)
    size = sum(a.size * a.dtype.itemsize for a in args)
    cost = pl.CostEstimate(flops=0, transcendentals=0, bytes_accessed=2 * size) if work else None
    spaces = [pltpu.HBM] * fetched + [pltpu.VMEM] * (len(args) - fetched)
    return pl.pallas_call(
        body,
        out_shape=outs,
        in_specs=[away] * fetched + [here] * (len(args) - fetched),
        out_specs=[here] * (len(outs) - sent) + [away] * sent,
        scratch_shapes=scratch,
        compiler_params=pltpu.CompilerParams(vmem_limit_bytes=16 << 20),
        cost_estimate=cost,
        input_output_aliases=same,
    )(*map(pltpu.with_memory_space_constraint, args, spaces))


def layer_sum(make, weight):
    n = lax.axis_size("layer")
    near_by, far_off = [[(i, i ^ span) for i in range(n)] for span in (1, n // 2 + 1)]
    theirs = lax.ppermute(make(True), "layer", near_by)
    mine = make(False)
    [pair] = call(add, [near(mine.shape, half)], mine, theirs)
    [turned] = call(turn, [near(weight.shape[::-1], half)], weight, pair, work=True)
    far = lax.ppermute(pair, "layer", far_off)
    [far] = call(lambda *refs: None, [near(far.shape, half)], turned, far, same={1: 0})
    back = [lax.ppermute(x, "layer", near_by) for x in (pair, far)]
    return (back[0], far), (pair, back[1]), turned


def features(other, width):
    which = lax.rem(lax.axis_index("layer") + int(other), 2)
    return pl.ds(pl.multiple_of(which * width, width), width)


def trade(pieces):
    n, came = lax.axis_size("feat"), list(pieces)
    for k in reversed(range(1, n // 2)):
        came[k] = lax.ppermute(pieces[k], "feat", [(i, i ^ k) for i in range(n)])
    return came


def mirror(block):
    n = lax.axis_size("feat")
    return lax.ppermute(block, "feat", [(i, (i + n // 2) % n) for i in range(n)])


def in_first_half():
    return lax.axis_index("feat") < lax.axis_size("feat") // 2


def place():
    return lax.rem(lax.axis_index("feat"), lax.axis_size("feat") // 2)


def nearest_last(came):
    return [came[0], *came[:0:-1]]


def last(came):
    return [came[0], *came[:2:-1], *came[1:3]]


def stack(refs):
    return jnp.concatenate([ref[...] for ref in refs])


def sum_of(refs):
    return functools.reduce(lambda so_far, ref: so_far + ref[...].astype(wide), refs[1:], refs[0][...].astype(wide))


def own_and_mirror(pair):
    rows = pair.shape[0] // 2
    first, low, high = in_first_half(), pair[:rows], pair[rows:]
    return jnp.where(first, low, high), jnp.where(first, high, low)


def add(one, other, out):
    out[...] = (one[...].astype(wide) + other[...].astype(wide)).astype(half)


def bring(*refs):
    *refs, done = refs
    n = len(refs) // 2
    moves = [pltpu.make_async_copy(refs[i], refs[n + i], done.at[i]) for i in range(n)]
    for move in moves:
        move.start()
    for move in moves:
        move.wait()


def join(acts, other, pair):
    first = in_first_half()
    mine, theirs = acts[...].astype(wide), other[...].astype(wide)
    both = [jnp.where(first, mine, theirs), jnp.where(first, theirs, mine)]
    pair[...] = jnp.concatenate(both).astype(half)


def encode(other, weight, *rest):
    *groups, out = rest
    x = stack(groups)
    first = features(other, out.shape[1]).start
    for at in range(0, out.shape[1], columns):
        there = pl.ds(pl.multiple_of(first + at, columns), columns)
        out[:, at : at + columns] = jnp.dot(x, weight[:, there], preferred_element_type=wide).astype(out.dtype)


def turn(weight, after, out):
    for at in range(0, weight.shape[0], columns):
        out[:, at : at + columns] = weight[at : at + columns, :].T


def spread_rows(x, weight, rows_in, so_far, outs):
    for at in range(0, weight.shape[1], columns):
        there = slice(at, at + columns)
        found = jnp.dot(x, weight[rows_in, there], preferred_element_type=wide)
        if so_far is None:
            outs[0][:, there] = found
            continue
        found = (found + so_far[:, there]).astype(half)
        for k, out in enumerate(outs):
            rows = out.shape[0]
            out[:, there] = found[k * rows : (k + 1) * rows]


def decode(last, terms, others, enc_bias, threshold, weight, before, slope, *outs):
    which = features(not last, terms.shape[1])
    preact = terms[...].astype(wide) + others[...].astype(wide) + enc_bias[:, which]
    gating = jax.nn.sigmoid((preact - threshold[:, which]) / jump_scale)
    slope[...] = gating + preact * gating * (1.0 - gating) / jump_scale
    spread_rows((preact * gating).astype(half), weight, which, before if last else None, outs)


def decode_grad(last, terms, others, slope, weight, before, total, *outs):
    latent_grad = terms[...].astype(wide) + others[...].astype(wide)
    n, me = lax.axis_size("feat"), place()
    rows = total.shape[0] // n
    for i in range(n):
        block = lax.bitwise_xor(me, i // 2) + i % 2 * (n // 2)
        total[pl.ds(pl.multiple_of(block * rows, rows), rows), :] = latent_grad[i * rows : (i + 1) * rows]
    x = (latent_grad * slope[...]).astype(half)
    spread_rows(x, weight, features(not last, terms.shape[1]), before if last else None, outs)


def add_pair(*refs):
    *terms, out, sent = refs
    found = sum_of(terms)
    out[...] = found
    sent[...] = found.astype(half)


def add_last(*refs):
    *terms, out, sent = refs
    mine, theirs = own_and_mirror(sum_of(terms))
    out[...] = mine
    sent[...] = theirs.astype(half)


def compare(one, other, dec_bias, acts, token_mask, error, pair, squared):
    rows, tokens = error.shape[0], token_mask.shape[1]
    row = lax.broadcasted_iota(jnp.int32, (2 * rows, tokens), 0)
    token = place() * rows + jnp.where(row < rows, row, tokens // 2 + row - rows)
    own = token == lax.broadcasted_iota(jnp.int32, (2 * rows, tokens), 1)
    mask = jnp.sum(jnp.where(own, token_mask[...].astype(wide), 0.0), axis=1, keepdims=True)
    both = mask * (one[...] + other[...].astype(wide) + dec_bias[...] - acts[...].astype(wide))
    pair[...] = both.astype(half)
    found, _ = own_and_mirror(both)
    error[...] = found
    means = jnp.mean(found * found, axis=1, keepdims=True)
    same = lax.broadcasted_iota(jnp.int32, (rows, rows), 0) == lax.broadcasted_iota(jnp.int32, (rows, rows), 1)
    squared[...] = jnp.sum(jnp.where(same, means, 0.0), axis=0, keepdims=True)


def leave(grad, grad_other, squared, grad_out, squared_out, done):
    mine, theirs = [grad_out.at[:, features(which, grad.shape[1])] for which in (True, False)]
    moves = [(grad, mine), (grad_other, theirs), (squared, squared_out)]
    moves = [pltpu.make_async_copy(here, there, done.at[i]) for i, (here, there) in enumerate(moves)]
    for move in moves:
        move.start()
    for move in moves:
        move.wait()


def finish(one, other, error, out):
    out[...] = (one[...] + other[...].astype(wide) - error[...]).astype(half)


def shards(activations, enc_weight, dec_weight, enc_bias, threshold, dec_bias, token_mask):
    n_feat = lax.axis_size("feat")
    tok_dev, _, depth = activations.shape
    tokens, width, groups = n_feat * tok_dev, enc_bias.shape[0], n_feat // 2
    enc, dec = enc_weight[0], dec_weight[0]
    acts = activations[:, 0]
    own, pair = (tok_dev, depth), (2 * tok_dev, depth)

    other = mirror(acts)
    far = (acts, enc_bias[None], threshold[None])
    acts, enc_bias, threshold = call(
        bring,
        [near(x.shape, x.dtype) for x in far],
        *far,
        scratch=[pltpu.SemaphoreType.DMA((len(far),))],
        fetched=len(far),
        work=True,
    )
    [acts_pair] = call(join, [near(pair, half)], acts, other)
    [acts_pair] = call(lambda *refs: None, [near(pair, half)], enc, dec, acts_pair, fetched=2, same={2: 0})
    groups_of = trade([acts_pair] * groups)
    [sent] = call(functools.partial(encode, True), [near((tokens, width // 2), half)], enc, *groups_of)
    kept = lambda weight, given: call(
        functools.partial(encode, False), [near((tokens, width // 2), wide)], weight, *given
    )[0]
    mine, theirs, dec_turned = layer_sum(lambda other: sent if other else kept(enc, groups_of), dec)
    by_feature, whole = near((tokens, width // 2), wide), near((tokens, depth), wide)
    by_group = [near(pair, half)] * groups
    given = (enc_bias, threshold, dec)
    slope, part = call(functools.partial(decode, False), [by_feature, whole], *mine, *given, dec_turned)
    slope_other, *decoded = call(functools.partial(decode, True), [by_feature, *by_group], *theirs, *given, part)
    one, other = call(add_pair, [near(pair, wide), near(pair, half)], *nearest_last(trade(decoded)))
    error, error_pair, squared = call(
        compare,
        [near(own, wide), near(pair, half), near((1, tok_dev), wide)],
        one,
        mirror(other),
        dec_bias,
        acts_pair,
        token_mask[None],
    )
    errors = trade([error_pair] * groups)
    [sent] = call(functools.partial(encode, True), [near((tokens, width // 2), half)], dec_turned, *errors)
    mine, theirs, enc_turned = layer_sum(lambda other: sent if other else kept(dec_turned, errors), enc)
    grad, part = call(functools.partial(decode_grad, False), [by_feature, whole], *mine, slope, enc_turned, sent)
    grad_other, *grads = call(
        functools.partial(decode_grad, True), [by_feature, *by_group], *theirs, slope_other, enc_turned, part
    )
    one, other = call(add_last, [near(own, wide), near(own, half)], *last(trade(grads)))
    latent_grad, squared = call(
        leave,
        [free((tokens, width), wide), free((1, tok_dev), wide)],
        grad,
        grad_other,
        squared,
        scratch=[pltpu.SemaphoreType.DMA((3,))],
        sent=2,
        work=True,
    )
    [input_grad] = call(finish, [free(own, half)], one, mirror(other), error)
    return (squared.T, latent_grad, input_grad[:, None])


def solution(mesh):
    return jax.shard_map(
        shards,
        mesh=mesh,
        in_specs=(
            P("feat", "layer", None),
            P("layer", None, "feat"),
            P("layer", "feat", None),
            P("feat"),
            P("feat"),
            P("layer", None),
            P(),
        ),
        out_specs=(P("feat", "layer"), P(None, "feat"), P("feat", "layer", None)),
        check_vma=False,
    )
```
